32 devices in a mesh: sess: 2 (over x), ctx: 16 (over z, y, core).
Axes of the slice: x: 2, y: 2, z: 4, core: 2. Of those that a mesh axis runs over, the one named last changes fastest.
Arguments:
- query_rows: bfloat16 [2, 1024, 4096], P('sess', 'ctx'), may hold values from -6 to 6
- key_rows: bfloat16 [2, 1024, 4096], P('sess', 'ctx'), may hold values from -6 to 6
- value_rows: bfloat16 [2, 1024, 4096], P('sess', 'ctx'), may hold values from -6 to 6
- seg_starts: int32 [2, 4], P('sess'), may hold values from 0 to 1023, as said below
- norm_gain: float32 [4096], replicated, may hold values from 0.1 to 1.9
Outputs:
- attended: bfloat16 [2, 1024, 4096], P('sess', 'ctx')
The draws below stay inside these ranges and needn't reach their ends.
Inputs may be any that keep to these rules, and one draw needn't show every extreme that they name: `seg_starts`: within each session the starts rise strictly, the first is 0 and the last is 1023.
All inputs are finite; a program needn't handle non-finite values.
Results may differ from the reference program's by a relative error of at most 0.0049.
Values sent between devices are 32-bit elements; how exact they have to be, the bound alone decides.
No kernel may reach another device: no remote copies, remote signals or barrier semaphores. Data moves between devices by JAX's collectives and lax.ppermute only.
A program may use at most 192 MiB of HBM per device.

```python
import jax
import jax.numpy as jnp
from jax import lax

HEADS = 32
HD = 128
TOK_DEV = 64
SEGS = 4
LENGTH = 1024
SESSIONS = 2


def draw_seg_starts(key, part):

    def one_row(row_key):
        inner = jax.random.permutation(row_key, LENGTH - 2)[:SEGS - 2] + 1
        picked = jnp.sort(inner.astype(jnp.int32))
        first = jnp.zeros((1,), jnp.int32)
        final = jnp.full((1,), LENGTH - 1, jnp.int32)
        return jnp.concatenate([first, picked, final]).astype(jnp.int32)
    row_keys = jax.random.split(jax.random.fold_in(key, 7), SESSIONS)
    return jax.vmap(one_row)(row_keys)


def block_levels(own_key, dims, cuts, low, largest):
    loudness, own = 1.0, jax.random.fold_in(own_key, 6)
    for position, parts in cuts:
        draws = jnp.exp(jax.random.uniform(jax.random.fold_in(own, position), (parts,), jnp.float32, low / len(cuts), largest / len(cuts)))
        loudness = loudness * jnp.repeat(draws, dims[position] // parts).reshape([-1 if axis == position else 1 for axis in range(len(dims))])
    return loudness


def noise(rng, extent, deviation, bound, cuts=(), kind=jnp.bfloat16):
    loudness = block_levels(rng, extent, cuts, -0.22, 0.18) if cuts else 1.0
    array = jax.random.normal(rng, extent, jnp.float32) * deviation * loudness
    return jnp.minimum(jnp.maximum(array, -bound), bound).astype(kind)


def setup_inputs(seed: int = 0) -> dict:
    arg_keys = jax.random.split(jax.random.key(seed), 6)
    return {
        "query_rows": noise(arg_keys[0], (SESSIONS, LENGTH, HEADS * HD), 1.0, 6.0, ((0, 2), (1, 16))),
        "key_rows": noise(arg_keys[1], (SESSIONS, LENGTH, HEADS * HD), 1.0, 6.0, ((0, 2), (1, 16))),
        "value_rows": noise(arg_keys[2], (SESSIONS, LENGTH, HEADS * HD), 1.0, 6.0, ((0, 2), (1, 16))),
        "seg_starts": draw_seg_starts(jax.random.fold_in(arg_keys[5], 71), 0),
        "norm_gain": jnp.clip(1.0 + 0.18 * jax.random.normal(arg_keys[4], (HEADS * HD,), jnp.float32), 0.1, 1.9),
    }


def one_session(packed):
    query_rows, key_rows, value_rows, start_list = packed
    blocks = LENGTH // TOK_DEV
    positions = jnp.arange(LENGTH, dtype=jnp.int32)
    seg_ids = lax.optimization_barrier(jnp.sum((start_list[None, :] <= positions[:, None]).astype(jnp.int32), axis=1))
    query_blocks = query_rows.reshape(blocks, TOK_DEV, HEADS, HD)
    key_blocks = key_rows.reshape(blocks, TOK_DEV, HEADS, HD)
    value_blocks = value_rows.reshape(blocks, TOK_DEV, HEADS, HD)
    seg_blocks = seg_ids.reshape(blocks, TOK_DEV)
    causal = jnp.arange(TOK_DEV)[:, None] >= jnp.arange(TOK_DEV)[None, :]

    def step(state, inputs):
        query_b, key_b, value_b, seg_b, index = inputs
        block_start = (index * TOK_DEV).astype(jnp.int32)
        prior_count = jnp.sum((start_list < block_start).astype(jnp.int32))
        query_f = query_b.astype(jnp.float32)
        key_f = key_b.astype(jnp.float32)
        value_f = value_b.astype(jnp.float32)
        scores = jnp.einsum('the,uhe->htu', query_f, key_f)
        allowed = causal & (seg_b[:, None] == seg_b[None, :])
        weights = jnp.where(allowed[None], scores, 0.0).astype(jnp.bfloat16)
        intra = jnp.einsum('htu,uhe->the', weights.astype(jnp.float32), value_f)
        carried = state.astype(jnp.bfloat16).astype(jnp.float32)
        inter = jnp.einsum('the,hef->thf', query_f, carried)
        use_mask = (seg_b == prior_count).astype(jnp.float32)
        mixed = (intra + use_mask[:, None, None] * inter).reshape(TOK_DEV, HEADS * HD)
        last_seg = seg_b[-1]
        keep_mask = (seg_b == last_seg).astype(jnp.float32)
        summary = jnp.einsum('uhe,uhf->hef', key_f * keep_mask[:, None, None], value_f)
        reset_flag = (last_seg != prior_count).astype(jnp.float32)
        new_state = (1.0 - reset_flag) * state + summary
        return (new_state, mixed)
    initial = jnp.zeros((HEADS, HD, HD), jnp.float32)
    indices = jnp.arange(blocks, dtype=jnp.int32)
    final_state, mixed_all = lax.scan(step, initial, (query_blocks, key_blocks, value_blocks, seg_blocks, indices))
    return mixed_all.reshape(LENGTH, HEADS * HD)

def reference(query_rows, key_rows, value_rows, seg_starts, norm_gain):
    mixed = lax.map(one_session, (query_rows, key_rows, value_rows, seg_starts))
    scale_inv = lax.rsqrt(lax.optimization_barrier(jnp.mean(mixed * mixed, axis=-1, keepdims=True)) + 1e-05)
    return (mixed * scale_inv * norm_gain).astype(jnp.bfloat16)
```

```python
import functools

import jax
import jax.numpy as jnp
from jax import lax
from jax.experimental import pallas as pl
from jax.experimental.pallas import tpu as pltpu
from jax.sharding import PartitionSpec as P

HD = 128
CHIPS = 4
F32 = jnp.float32
BF16 = jnp.bfloat16
VM = pl.BlockSpec(memory_space=pltpu.VMEM)
SM = pl.BlockSpec(memory_space=pltpu.SMEM)
PARAMS = pltpu.CompilerParams(vmem_limit_bytes=32 * 1024 * 1024)


def place():
    block = lax.axis_index("ctx")
    return block % 2, (block // 2) % CHIPS, block // (2 * CHIPS), block


def segment_at(starts, position):
    count = jnp.int32(0)
    for i in range(starts.shape[1]):
        count = count + (starts[0, i] <= position).astype(jnp.int32)
    return count


def same(starts, rows, late, early):
    one = segment_at(starts, (late + 1) * rows - 1)
    two = segment_at(starts, (early + 1) * rows - 1)
    return (one == two).astype(F32)


def column(head):
    return pl.ds(pl.multiple_of(head * HD, HD), HD)


def segment_rows(starts, positions):
    count = jnp.zeros(positions.shape, jnp.int32)
    for i in range(starts.shape[1]):
        count = count + (starts[0, i] <= positions).astype(jnp.int32)
    return count


def head_of(core, chip, step, quarter):
    which = lax.bitwise_xor(chip, step // quarter)
    return core * CHIPS * quarter + which * quarter + step % quarter


def summary_kernel(starts, key_ref, value_ref, send_ref, keep_ref):
    core, chip, _, block = place()
    rows, width = key_ref.shape
    half = width // HD // 2
    begin = block * rows
    last = segment_at(starts, begin + rows - 1)
    positions = begin + lax.broadcasted_iota(jnp.int32, (rows, HD), 0)
    kept = segment_rows(starts, positions) == last
    for out, which in ((send_ref, 1 - core), (keep_ref, core)):
        for step in range(half):
            at = column(head_of(which, chip, step, half // CHIPS))
            key = jnp.where(kept, key_ref[:, at].astype(F32), 0.0).astype(BF16)
            out[step * HD:(step + 1) * HD, :] = lax.dot_general(
                key, value_ref[:, at], (((0,), (0,)), ((), ())), preferred_element_type=F32)


def chip_kernel(starts, rows, keep_ref, got_ref, *pieces):
    core, _, _, block = place()
    joined = same(starts, rows, block // 2 * 2 + 1, block // 2 * 2)
    mine = jnp.where(core == 0, joined, 1.0)
    other = jnp.where(core == 0, 1.0, joined)
    size = pieces[0].shape[0]
    for k, piece in enumerate(pieces):
        at = slice(k * size, (k + 1) * size)
        piece[...] = mine * keep_ref[at, :] + other * got_ref[at, :]


def total_kernel(starts, rows, *refs):
    pieces, out = refs[:-1], refs[-1]
    _, chip, group, _ = place()
    first = group * 2 * CHIPS
    total = None
    for k, piece in enumerate(pieces):
        block = first + 2 * lax.bitwise_xor(chip, k) + 1
        term = same(starts, rows, first + 2 * CHIPS - 1, block) * piece[...]
        total = term if total is None else total + term
    out[...] = total


def carry_kernel(starts, rows, shifts, *refs):
    pieces, groups, outs = refs[:CHIPS], refs[CHIPS:CHIPS + shifts], refs[CHIPS + shifts:]
    _, chip, group, _ = place()
    first = group * 2 * CHIPS
    before = None
    for s, total in enumerate(groups):
        block = first - 1 - s * 2 * CHIPS
        term = jnp.where(block >= 0, same(starts, rows, first - 1, block), 0.0) * total[...]
        before = term if before is None else before + term
    for k, out in enumerate(outs):
        target = lax.bitwise_xor(chip, k)
        end = first + 2 * target - 1
        state = same(starts, rows, end, first - 1) * before
        for j, piece in enumerate(pieces):
            source = lax.bitwise_xor(chip, j)
            use = jnp.where(source < target, same(starts, rows, end, first + 2 * source + 1), 0.0)
            state = state + use * piece[...]
        out[...] = state


def pair_kernel(starts, rows, keep_ref, *refs):
    pieces, out = refs[:-1], refs[-1]
    core, _, _, block = place()
    joined = same(starts, rows, block, block - 1)
    scale = jnp.where(core == 0, joined, 1.0)
    add = jnp.where(core == 0, 1.0, 0.0)
    size = pieces[0].shape[0]
    for k, piece in enumerate(pieces):
        at = slice(k * size, (k + 1) * size)
        out[at, :] = scale * piece[...] + add * keep_ref[at, :]


def intra_kernel(starts, query_ref, key_ref, value_ref, out_ref):
    _, _, _, block = place()
    rows, width = query_ref.shape
    begin = block * rows
    late = begin + lax.broadcasted_iota(jnp.int32, (rows, rows), 0)
    early = begin + lax.broadcasted_iota(jnp.int32, (rows, rows), 1)
    allowed = (late >= early) & (segment_rows(starts, late) == segment_rows(starts, early))
    for head in range(width // HD):
        at = slice(head * HD, (head + 1) * HD)
        scores = lax.dot_general(
            query_ref[:, at], key_ref[:, at], (((1,), (1,)), ((), ())), preferred_element_type=F32)
        weights = jnp.where(allowed, scores, 0.0).astype(BF16)
        out_ref[:, at] = jnp.dot(weights, value_ref[:, at], preferred_element_type=F32)


def final_kernel(starts, query_ref, intra_ref, gain_ref, got_ref, sibling_ref, *refs):
    pieces, out_ref, mixed = refs[:CHIPS], refs[CHIPS], refs[CHIPS + 1]
    core, chip, _, block = place()
    rows, width = query_ref.shape
    half = width // HD // 2
    quarter = half // CHIPS
    begin = block * rows
    prior = segment_at(starts, begin - 1)
    positions = begin + lax.broadcasted_iota(jnp.int32, (rows, HD), 0)
    use = (segment_rows(starts, positions) == prior).astype(F32)
    joined = same(starts, rows, block - 1, block - 2)
    scale = jnp.where(core == 0, 1.0, joined)
    add = jnp.where(core == 0, 0.0, 1.0)
    squares = jnp.zeros((rows, HD), F32)
    for own in (True, False):
        which = core if own else 1 - core
        for step in range(half):
            at = column(head_of(which, chip, step, quarter))
            if own:
                part = (step % quarter) * HD
                state = scale * pieces[step // quarter][part:part + HD, :]
                state = state + add * got_ref[step * HD:(step + 1) * HD, :]
            else:
                state = sibling_ref[step * HD:(step + 1) * HD, :]
            inter = jnp.dot(query_ref[:, at], state.astype(BF16), preferred_element_type=F32)
            both = intra_ref[:, at] + use * inter
            mixed[:, at] = both
            squares = squares + both * both
    mean = jnp.sum(squares, axis=-1, keepdims=True) * (1.0 / width)
    norm = jnp.broadcast_to(lax.rsqrt(mean + 1e-05), (rows, HD))
    for head in range(width // HD):
        at = slice(head * HD, (head + 1) * HD)
        out_ref[:, at] = (mixed[:, at] * norm * gain_ref[:, at]).astype(BF16)


def arrays(shape, count, dtype=F32):
    return [jax.ShapeDtypeStruct(shape, dtype)] * count


def shards(count, query_rows, key_rows, value_rows, seg_starts, norm_gain):
    query, key, value = query_rows[0], key_rows[0], value_rows[0]
    rows, width = query.shape
    tall = width // 2
    groups = count // (2 * CHIPS)

    def call(kernel, outs, *args, scratch=()):
        return pl.pallas_call(
            kernel, out_shape=outs, in_specs=[SM] + [VM] * len(args),
            out_specs=jax.tree.map(lambda _: VM, outs), scratch_shapes=scratch, compiler_params=PARAMS,
        )(seg_starts, *args)

    def swap(array, bits):
        return lax.ppermute(array, "ctx", [(i, i ^ bits) for i in range(count)])

    send, keep = call(summary_kernel, arrays((tall, HD), 2), key, value)
    got = swap(send, 1)
    intra = call(intra_kernel, arrays((rows, width), 1)[0], query, key, value)
    lane = (tall // CHIPS, HD)
    own = call(lambda s, *r: chip_kernel(s, rows, *r), arrays(lane, CHIPS), keep, got)
    pieces = [own[0]] + [swap(own[k], 2 * k) for k in range(1, CHIPS)]
    total = call(lambda s, *r: total_kernel(s, rows, *r), arrays(lane, 1)[0], *pieces)
    before = [
        lax.ppermute(total, "ctx", [(i, i + shift * 2 * CHIPS) for i in range(count - shift * 2 * CHIPS)])
        for shift in range(1, groups)
    ]
    outs = call(lambda s, *r: carry_kernel(s, rows, groups - 1, *r), arrays(lane, CHIPS), *pieces, *before)
    states = [outs[0]] + [swap(outs[k], 2 * k) for k in range(1, CHIPS)]
    sibling = swap(call(lambda s, *r: pair_kernel(s, rows, *r), arrays((tall, HD), 1)[0], keep, *states), 1)
    attended = call(
        final_kernel, jax.ShapeDtypeStruct((rows, width), BF16), query, intra, norm_gain[None, :], got, sibling,
        *states, scratch=[pltpu.VMEM((rows, width), F32)])
    return attended[None]


def solution(mesh):
    placed = (
        P("sess", "ctx", None),
        P("sess", "ctx", None),
        P("sess", "ctx", None),
        P("sess", None),
        P(),
    )
    return jax.shard_map(
        functools.partial(shards, mesh.shape["ctx"]), mesh=mesh, in_specs=placed,
        out_specs=P("sess", "ctx", None), check_vma=False
    )
```

```python
import functools

import jax
import jax.numpy as jnp
from jax import lax
from jax.experimental import pallas as pl
from jax.experimental.pallas import tpu as pltpu
from jax.sharding import PartitionSpec as P

HD = 128
PARTS = 2
CHIPS = 4
F32 = jnp.float32
BF16 = jnp.bfloat16
VM = pl.BlockSpec(memory_space=pltpu.VMEM)
HB = pl.BlockSpec(memory_space=pltpu.HBM)
SM = pl.BlockSpec(memory_space=pltpu.SMEM)
PARAMS = pltpu.CompilerParams(vmem_limit_bytes=32 * 1024 * 1024)


def place():
    block = lax.axis_index("ctx")
    return block % 2, (block // 2) % CHIPS, block // (2 * CHIPS), block


def segment_at(starts, position):
    count = jnp.int32(0)
    for i in range(starts.shape[1]):
        count = count + (starts[0, i] <= position).astype(jnp.int32)
    return count


def same(starts, rows, late, early):
    one = segment_at(starts, (late + 1) * rows - 1)
    two = segment_at(starts, (early + 1) * rows - 1)
    return (one == two).astype(F32)


def column(head):
    return pl.ds(pl.multiple_of(head * HD, HD), HD)


def segment_rows(starts, positions):
    count = jnp.zeros(positions.shape, jnp.int32)
    for i in range(starts.shape[1]):
        count = count + (starts[0, i] <= positions).astype(jnp.int32)
    return count


def head_of(core, chip, step, quarter):
    which = lax.bitwise_xor(chip, step // quarter)
    return core * CHIPS * quarter + which * quarter + step % quarter


def summarize(starts, key_ref, value_ref, half, out):
    _, chip, _, block = place()
    rows, width = key_ref.shape
    steps = width // HD // 2
    begin = block * rows
    last = segment_at(starts, begin + rows - 1)
    positions = begin + lax.broadcasted_iota(jnp.int32, (rows, HD), 0)
    kept = segment_rows(starts, positions) == last
    for step in range(steps):
        at = column(head_of(half, chip, step, steps // CHIPS))
        key = jnp.where(kept, key_ref[:, at].astype(F32), 0.0).astype(BF16)
        out[step * HD:(step + 1) * HD, :] = lax.dot_general(
            key, value_ref[:, at], (((0,), (0,)), ((), ())), preferred_element_type=F32)


def send_kernel(starts_hbm, key_hbm, value_hbm, send_ref, key_ref, value_ref, starts, sems):
    copies = [
        pltpu.make_async_copy(source, target, sems.at[i])
        for i, (source, target) in enumerate(((starts_hbm, starts), (key_hbm, key_ref), (value_hbm, value_ref)))
    ]
    for copy in copies:
        copy.start()
    for copy in copies:
        copy.wait()
    summarize(starts, key_ref, value_ref, 1 - place()[0], send_ref)


def keep_kernel(starts, key_ref, value_ref, keep_ref):
    summarize(starts, key_ref, value_ref, place()[0], keep_ref)


def chip_kernel(part, starts, rows, keep_ref, got_ref, *refs):
    pieces = refs[-CHIPS:]
    core, _, _, block = place()
    joined = same(starts, rows, block // 2 * 2 + 1, block // 2 * 2)
    mine = jnp.where(core == 0, joined, 1.0)
    other = jnp.where(core == 0, 1.0, joined)
    size = pieces[0].shape[0]
    for k, piece in enumerate(pieces):
        begin = (k * PARTS + part) * size
        at = slice(begin, begin + size)
        piece[...] = mine * keep_ref[at, :] + other * got_ref[at, :]


def total_kernel(starts, rows, *refs):
    pieces, out = refs[:CHIPS], refs[-1]
    _, chip, group, _ = place()
    first = group * 2 * CHIPS
    total = None
    for k, piece in enumerate(pieces):
        block = first + 2 * lax.bitwise_xor(chip, k) + 1
        term = same(starts, rows, first + 2 * CHIPS - 1, block) * piece[...]
        total = term if total is None else total + term
    out[...] = total


def carry_kernel(starts, rows, shifts, *refs):
    pieces, groups, outs = refs[:CHIPS], refs[CHIPS:CHIPS + shifts], refs[CHIPS + shifts:]
    _, chip, group, _ = place()
    first = group * 2 * CHIPS
    before = None
    for s, total in enumerate(groups):
        block = first - 1 - s * 2 * CHIPS
        term = jnp.where(block >= 0, same(starts, rows, first - 1, block), 0.0) * total[...]
        before = term if before is None else before + term
    for k, out in enumerate(outs):
        target = lax.bitwise_xor(chip, k)
        end = first + 2 * target - 1
        state = same(starts, rows, end, first - 1) * before
        for j, piece in enumerate(pieces):
            source = lax.bitwise_xor(chip, j)
            use = jnp.where(source < target, same(starts, rows, end, first + 2 * source + 1), 0.0)
            state = state + use * piece[...]
        out[...] = state


def pair_kernel(starts, rows, keep_ref, *refs):
    pieces, out = refs[:-1], refs[-1]
    core, _, _, block = place()
    joined = same(starts, rows, block, block - 1)
    scale = jnp.where(core == 0, joined, 1.0)
    add = jnp.where(core == 0, 1.0, 0.0)
    size = pieces[0].shape[0]
    for part in range(PARTS):
        for k in range(CHIPS):
            begin = (k * PARTS + part) * size
            at = slice(begin, begin + size)
            out[at, :] = scale * pieces[part * CHIPS + k][...] + add * keep_ref[at, :]


def intra_kernel(heads, starts, query_ref, key_ref, value_ref, *refs):
    out_ref = refs[-1]
    _, _, _, block = place()
    rows = query_ref.shape[0]
    begin = block * rows
    late = begin + lax.broadcasted_iota(jnp.int32, (rows, rows), 0)
    early = begin + lax.broadcasted_iota(jnp.int32, (rows, rows), 1)
    allowed = (late >= early) & (segment_rows(starts, late) == segment_rows(starts, early))
    for place_out, head in enumerate(heads):
        at = slice(head * HD, (head + 1) * HD)
        scores = lax.dot_general(
            query_ref[:, at], key_ref[:, at], (((1,), (1,)), ((), ())), preferred_element_type=F32)
        weights = jnp.where(allowed, scores, 0.0).astype(BF16)
        out_ref[:, place_out * HD:(place_out + 1) * HD] = jnp.dot(
            weights, value_ref[:, at], preferred_element_type=F32)


def final_kernel(starts, query_ref, gain_ref, got_ref, sibling_ref, *refs):
    intra_refs, pieces, (out_ref, mixed) = refs[:2], refs[2:2 + CHIPS * PARTS], refs[2 + CHIPS * PARTS:]
    core, chip, _, block = place()
    rows, width = query_ref.shape
    half = width // HD // 2
    quarter = half // CHIPS
    begin = block * rows
    prior = segment_at(starts, begin - 1)
    positions = begin + lax.broadcasted_iota(jnp.int32, (rows, HD), 0)
    use = (segment_rows(starts, positions) == prior).astype(F32)
    joined = same(starts, rows, block - 1, block - 2)
    scale = jnp.where(core == 0, 1.0, joined)
    add = jnp.where(core == 0, 0.0, 1.0)
    squares = jnp.zeros((rows, HD), F32)
    for own in (True, False):
        which = core if own else 1 - core
        for step in range(half):
            at = column(head_of(which, chip, step, quarter))
            if own:
                size = quarter // PARTS
                piece = pieces[step % quarter // size * CHIPS + step // quarter]
                begin = step % size * HD
                state = scale * piece[begin:begin + HD, :]
                state = state + add * got_ref[step * HD:(step + 1) * HD, :]
            else:
                state = sibling_ref[step * HD:(step + 1) * HD, :]
            mixed[:, at] = use * jnp.dot(query_ref[:, at], state.astype(BF16), preferred_element_type=F32)
    for head in range(width // HD):
        at = slice(head * HD, (head + 1) * HD)
        both = mixed[:, at] + intra_refs[head // half][:, head % half * HD:(head % half + 1) * HD]
        mixed[:, at] = both
        squares = squares + both * both
    mean = jnp.sum(squares, axis=-1, keepdims=True) * (1.0 / width)
    norm = jnp.broadcast_to(lax.rsqrt(mean + 1e-05), (rows, HD))
    for head in range(width // HD):
        at = slice(head * HD, (head + 1) * HD)
        out_ref[:, at] = (mixed[:, at] * norm * gain_ref[:, at]).astype(BF16)


def in_hbm(array):
    return pltpu.with_memory_space_constraint(array, pltpu.HBM)


def arrays(shape, count, dtype=F32):
    return [jax.ShapeDtypeStruct(shape, dtype)] * count


def shards(count, query_rows, key_rows, value_rows, seg_starts, norm_gain):
    query, key, value = query_rows[0], key_rows[0], value_rows[0]
    rows, width = query.shape
    tall = width // 2
    groups = count // (2 * CHIPS)

    def call(kernel, outs, *args, scratch=()):
        return pl.pallas_call(
            kernel, out_shape=outs, in_specs=[SM] + [VM] * len(args),
            out_specs=jax.tree.map(lambda _: VM, outs), scratch_shapes=scratch, compiler_params=PARAMS,
        )(seg_starts, *args)

    def swap(array, bits):
        return lax.ppermute(array, "ctx", [(i, i ^ bits) for i in range(count)])

    tall_array = arrays((tall, HD), 1)[0]
    send, key, value = pl.pallas_call(
        send_kernel, out_shape=[tall_array] + arrays((rows, width), 2, BF16), in_specs=[HB] * 3, out_specs=[VM] * 3,
        scratch_shapes=[pltpu.SMEM(seg_starts.shape, jnp.int32), pltpu.SemaphoreType.DMA((3,))],
        compiler_params=PARAMS,
    )(in_hbm(seg_starts), in_hbm(key), in_hbm(value))
    got = swap(send, 1)
    keep = call(keep_kernel, tall_array, key, value)
    lanes = arrays((tall // CHIPS // PARTS, HD), CHIPS)
    parts, befores, states = [], [], []
    after = []
    for part in range(PARTS):
        own = call(lambda s, *r: chip_kernel(part, s, rows, *r), lanes, keep, got, *after)
        pieces = [own[0]] + [swap(own[k], 2 * k) for k in range(1, CHIPS)]
        after = [pieces[1]]
        parts.append(pieces)
    heads = width // HD

    def inside(this, *after):
        span = range(this * heads // 2, (this + 1) * heads // 2)
        return call(functools.partial(intra_kernel, span), arrays((rows, width // 2), 1)[0], query, key, value, *after)

    after, intra = [], []
    for pieces in parts:
        total = call(lambda s, *r: total_kernel(s, rows, *r), lanes[0], *pieces, *after)
        if not after:
            intra.append(inside(0, total))
            after = intra
        befores.append([
            lax.ppermute(total, "ctx", [(i, (i + shift * 2 * CHIPS) % count) for i in range(count)])
            for shift in range(1, groups)
        ])
    for pieces, before in zip(parts, befores):
        outs = call(lambda s, *r: carry_kernel(s, rows, groups - 1, *r), lanes, *pieces, *before)
        states += [outs[0]] + [swap(outs[k], 2 * k) for k in range(1, CHIPS)]
    intra.append(inside(1, outs[0]))
    sibling = swap(call(lambda s, *r: pair_kernel(s, rows, *r), tall_array, keep, *states, intra[1]), 1)
    attended = call(
        final_kernel, jax.ShapeDtypeStruct((rows, width), BF16), query, norm_gain[None, :], got, sibling, *intra,
        *states, scratch=[pltpu.VMEM((rows, width), F32)])
    return attended[None]


def solution(mesh):
    placed = (
        P("sess", "ctx", None),
        P("sess", "ctx", None),
        P("sess", "ctx", None),
        P("sess", None),
        P(),
    )
    return jax.shard_map(
        functools.partial(shards, mesh.shape["ctx"]), mesh=mesh, in_specs=placed,
        out_specs=P("sess", "ctx", None), check_vma=False
    )
```

```python
import functools

import jax
import jax.numpy as jnp
from jax import lax
from jax.experimental import pallas as pl
from jax.experimental.pallas import tpu as pltpu
from jax.sharding import PartitionSpec as P

HD = 128
CHIPS = 4
SPLIT = (1, 1)
EARLY = (1, 2)
F32 = jnp.float32
BF16 = jnp.bfloat16
HB = pl.BlockSpec(memory_space=pltpu.HBM)
SM = pl.BlockSpec(memory_space=pltpu.SMEM)
VM = pl.BlockSpec(memory_space=pltpu.VMEM)
PARAMS = pltpu.CompilerParams(vmem_limit_bytes=32 * 1024 * 1024)


def place():
    block = lax.axis_index("ctx")
    return block % 2, (block // 2) % CHIPS, block // (2 * CHIPS), block


def segment_at(starts, position):
    count = jnp.int32(0)
    for i in range(starts.shape[1]):
        count = count + (starts[0, i] <= position).astype(jnp.int32)
    return count


def same(starts, rows, late, early):
    one = segment_at(starts, (late + 1) * rows - 1)
    two = segment_at(starts, (early + 1) * rows - 1)
    return (one == two).astype(F32)


def segment_rows(starts, positions):
    count = jnp.zeros(positions.shape, jnp.int32)
    for i in range(starts.shape[1]):
        count = count + (starts[0, i] <= positions).astype(jnp.int32)
    return count


def tile(index):
    return slice(index * HD, (index + 1) * HD)


def sizes(width):
    quarter = width // HD // 2 // CHIPS
    return [quarter * share // sum(SPLIT) for share in SPLIT]


def part_steps(width, part):
    return [(part, k, j) for k in range(CHIPS) for j in range(sizes(width)[part])]


def steps(width):
    return [(own, *step) for own in (True, False) for part in range(len(SPLIT)) for step in part_steps(width, part)]


def column(width, core, chip, own, part, k, j):
    parts = sizes(width)
    quarter = sum(parts)
    half = core if own else 1 - core
    head = (half * CHIPS + lax.bitwise_xor(chip, k)) * quarter + sum(parts[:part]) + j
    return pl.ds(pl.multiple_of(head * HD, HD), HD)


def table_rows(groups):
    names = ["chip_mine", "chip_other", "pair_scale", "pair_add", "mix_scale", "mix_add"]
    names += [("total", k) for k in range(CHIPS)]
    names += [("carry", k, j) for k in range(CHIPS) for j in range(CHIPS)]
    names += [("enter", k) for k in range(CHIPS)]
    names += [("before", s) for s in range(groups - 1)]
    return {name: i for i, name in enumerate(names)}


def weights(starts, rows, groups):
    core, chip, group, block = place()
    same_ = functools.partial(same, starts, rows)
    first = group * 2 * CHIPS
    joined = same_(block // 2 * 2 + 1, block // 2 * 2)
    after, mix = same_(block, block - 1), same_(block - 1, block - 2)
    found = {
        "chip_mine": jnp.where(core == 0, joined, 1.0),
        "chip_other": jnp.where(core == 0, 1.0, joined),
        "pair_scale": jnp.where(core == 0, after, 1.0),
        "pair_add": jnp.where(core == 0, 1.0, 0.0),
        "mix_scale": jnp.where(core == 0, 1.0, mix),
        "mix_add": jnp.where(core == 0, 0.0, 1.0),
    }
    for k in range(CHIPS):
        target = lax.bitwise_xor(chip, k)
        end = first + 2 * target - 1
        found["total", k] = same_(first + 2 * CHIPS - 1, first + 2 * target + 1)
        found["enter", k] = same_(end, first - 1)
        for j in range(CHIPS):
            source = lax.bitwise_xor(chip, j)
            found["carry", k, j] = jnp.where(source < target, same_(end, first + 2 * source + 1), 0.0)
    for s in range(groups - 1):
        block = first - 1 - s * 2 * CHIPS
        found["before", s] = jnp.where(block >= 0, same_(first - 1, block), 0.0)
    return found


def summarize(kept_ref, key_ref, value_ref, own, part, out):
    core, chip, _, _ = place()
    width = key_ref.shape[1]
    kept = kept_ref[...]
    for i, step in enumerate(part_steps(width, part)):
        at = column(width, core, chip, own, *step)
        out[tile(i), :] = lax.dot_general(
            key_ref[:, at] * kept, value_ref[:, at], (((0,), (0,)), ((), ())), preferred_element_type=F32)


def first_kernel(groups, starts_hbm, key_hbm, value_hbm, send_ref, key_ref, value_ref, table_ref, kept_ref, allowed_ref,
                 use_ref, starts, sems):
    copies = [
        pltpu.make_async_copy(source, target, sems.at[i])
        for i, (source, target) in enumerate(((starts_hbm, starts), (key_hbm, key_ref), (value_hbm, value_ref)))
    ]
    for copy in copies:
        copy.start()
    copies[0].wait()
    rows = key_ref.shape[0]
    _, _, _, block = place()
    begin = block * rows
    names = table_rows(groups)
    for name, weight in weights(starts, rows, groups).items():
        table_ref[names[name]:names[name] + 1, :] = jnp.full((1, HD), weight, F32)
    segments = segment_rows(starts, begin + lax.broadcasted_iota(jnp.int32, (rows, HD), 0))
    kept_ref[...] = (segments == segment_at(starts, begin + rows - 1)).astype(F32).astype(BF16)
    use_ref[...] = (segments == segment_at(starts, begin - 1)).astype(F32)
    late = begin + lax.broadcasted_iota(jnp.int32, (rows, rows), 0)
    early = begin + lax.broadcasted_iota(jnp.int32, (rows, rows), 1)
    allowed = (late >= early) & (segment_rows(starts, late) == segment_rows(starts, early))
    allowed_ref[...] = allowed.astype(F32)
    for copy in copies[1:]:
        copy.wait()
    summarize(kept_ref, key_ref, value_ref, False, 0, send_ref)


def summary_kernel(what, kept_ref, key_ref, value_ref, *outs):
    for (own, part), out in zip(what, outs):
        summarize(kept_ref, key_ref, value_ref, own, part, out)


def row(table_ref, groups, *name):
    at = table_rows(groups)[name if len(name) > 1 else name[0]]
    return table_ref[at:at + 1, :]


def chip_kernel(weight, keep_ref, got_ref, *refs):
    pieces = refs[-CHIPS:]
    size = pieces[0].shape[0]
    for k, piece in enumerate(pieces):
        at = slice(k * size, (k + 1) * size)
        piece[...] = weight("chip_mine") * keep_ref[at, :] + weight("chip_other") * got_ref[at, :]


def total_kernel(weight, *refs):
    pieces, out = refs[:CHIPS], refs[-1]
    total = None
    for k, piece in enumerate(pieces):
        term = weight("total", k) * piece[...]
        total = term if total is None else total + term
    out[...] = total


def carry_kernel(shifts, weight, *refs):
    pieces, groups, outs = refs[:CHIPS], refs[CHIPS:CHIPS + shifts], refs[-CHIPS:]
    before = None
    for s, total in enumerate(groups):
        term = weight("before", s) * total[...]
        before = term if before is None else before + term
    for k, out in enumerate(outs):
        state = weight("enter", k) * before
        for j, piece in enumerate(pieces):
            if j != k:
                state = state + weight("carry", k, j) * piece[...]
        out[...] = state


def pair_kernel(weight, keep_ref, *refs):
    pieces, out = refs[:CHIPS], refs[-1]
    size = pieces[0].shape[0]
    for k, piece in enumerate(pieces):
        at = slice(k * size, (k + 1) * size)
        out[at, :] = weight("pair_scale") * piece[...] + weight("pair_add") * keep_ref[at, :]


def intra_kernel(on, span, allowed_ref, query_ref, key_ref, value_ref, *refs):
    out_ref = refs[-1]
    core, chip, _, _ = place()
    width = query_ref.shape[1]

    def body():
        allowed = allowed_ref[...]
        for i, step in enumerate(steps(width)[slice(*span)]):
            at = column(width, core, chip, *step)
            scores = lax.dot_general(
                query_ref[:, at], key_ref[:, at], (((1,), (1,)), ((), ())), preferred_element_type=F32)
            out_ref[:, tile(i)] = jnp.dot(
                (scores * allowed).astype(BF16), value_ref[:, at], preferred_element_type=F32)

    if on is None:
        body()
    else:
        pl.when(core == on)(body)


def from_past(use, query_ref, step, state):
    core, chip, _, _ = place()
    at = column(query_ref.shape[1], core, chip, *step)
    return use * jnp.dot(query_ref[:, at], state.astype(BF16), preferred_element_type=F32)


def mix_kernel(cut, weight, use_ref, query_ref, *refs):
    parts = len(SPLIT)
    intras = refs[:4]
    refs = refs[4:]
    pieces, got_refs, sibling_refs = refs[:CHIPS * parts], refs[CHIPS * parts:][:parts], refs[CHIPS * parts + parts:-2]
    mixed_ref, squares_ref = refs[-2:]
    core, _, _, _ = place()
    rows, width = query_ref.shape
    use = use_ref[...]
    squares = jnp.zeros((rows, HD), F32)
    for i, step in enumerate(steps(width)):
        both = jnp.where(core == 0, intras[2 * (i >= cut)][:, tile(i - cut * (i >= cut))], intras[2 * (i >= cut) + 1][:, tile(i - cut * (i >= cut))])
        own, part, k, j = step
        at = tile(k * sizes(width)[part] + j)
        if own:
            state = weight("mix_scale") * pieces[part * CHIPS + k][tile(j), :] + weight("mix_add") * got_refs[part][at, :]
        elif part < parts - 1:
            state = sibling_refs[part][at, :]
        else:
            mixed_ref[:, tile(i)] = both
            continue
        both = both + from_past(use, query_ref, step, state)
        mixed_ref[:, tile(i)] = both
        squares = squares + both * both
    squares_ref[...] = squares


def norm_kernel(use_ref, query_ref, gain_ref, mixed_ref, squares_ref, sibling_ref, out_ref, last_ref):
    core, chip, _, _ = place()
    rows, width = query_ref.shape
    order = steps(width)
    first = len(order) - sibling_ref.shape[0] // HD
    use = use_ref[...]
    squares = squares_ref[...]
    for i, step in enumerate(order[first:]):
        both = mixed_ref[:, tile(first + i)] + from_past(use, query_ref, step, sibling_ref[tile(i), :])
        last_ref[:, tile(i)] = both
        squares = squares + both * both
    mean = jnp.sum(squares, axis=-1, keepdims=True) * (1.0 / width)
    norm = jnp.broadcast_to(lax.rsqrt(mean + 1e-05), (rows, HD))
    for i, step in enumerate(order):
        at = column(width, core, chip, *step)
        both = mixed_ref[:, tile(i)] if i < first else last_ref[:, tile(i - first)]
        out_ref[:, at] = (both * norm * gain_ref[:, at]).astype(BF16)


def in_hbm(array):
    return pltpu.with_memory_space_constraint(array, pltpu.HBM)


def array(shape, dtype=F32):
    return jax.ShapeDtypeStruct(shape, dtype)


def shards(count, query_rows, key_rows, value_rows, seg_starts, norm_gain):
    query, key, value = query_rows[0], key_rows[0], value_rows[0]
    rows, width = query.shape
    groups = count // (2 * CHIPS)
    parts = range(len(SPLIT))
    heads = len(steps(width))
    lanes = [[array((size * HD, HD))] * CHIPS for size in sizes(width)]
    talls = [array((CHIPS * size * HD, HD)) for size in sizes(width)]

    def call(kernel, outs, *args, scratch=()):
        return pl.pallas_call(
            kernel, out_shape=outs, in_specs=[VM] * len(args), out_specs=jax.tree.map(lambda _: VM, outs),
            scratch_shapes=scratch, compiler_params=PARAMS,
        )(*args)

    def weighted(kernel, outs, *args):
        def body(table_ref, *refs):
            return kernel(functools.partial(row, table_ref, groups), *refs)

        return call(body, outs, table, *args)

    def swap(what, bits):
        return lax.ppermute(what, "ctx", [(i, i ^ bits) for i in range(count)])

    def later(what, shift):
        return lax.ppermute(what, "ctx", [(i, (i + shift * 2 * CHIPS) % count) for i in range(count)])

    def exchange(own):
        return [own[0]] + [swap(own[k], 2 * k) for k in range(1, CHIPS)]

    def intra(on, span, *after):
        out = array((rows, (span[1] - span[0]) * HD))
        return call(functools.partial(intra_kernel, on, span), out, allowed, query, key, value, *after)

    table = array((-(-len(table_rows(groups)) // 8) * 8, HD))
    send, key, value, table, kept, allowed, use = pl.pallas_call(
        functools.partial(first_kernel, groups),
        out_shape=[talls[0]] + [array((rows, width), BF16)] * 2 + [
            table, array((rows, HD), BF16), array((rows, rows)), array((rows, HD))],
        in_specs=[HB] * 3, out_specs=[VM] * 7,
        scratch_shapes=[pltpu.SMEM(seg_starts.shape, jnp.int32), pltpu.SemaphoreType.DMA((3,))],
        compiler_params=PARAMS,
    )(in_hbm(seg_starts), in_hbm(key), in_hbm(value))
    gots, keeps = [], []
    for part in parts:
        gots.append(swap(send, 1))
        what = [(True, part)] + [(False, part + 1)][:len(SPLIT) - 1 - part]
        keep, *send = call(functools.partial(summary_kernel, what), [talls[p] for _, p in what], kept, key, value)
        keeps.append(keep)
        send = send[0] if send else None
    cut = heads * EARLY[0] // EARLY[1]
    zero = intra(0, (0, cut), keeps[0])
    pieces, befores, states, siblings = [], [], [], []
    after = [zero]
    for part in parts:
        own = weighted(chip_kernel, lanes[part], keeps[part], gots[part], *after)
        pieces.append(exchange(own))
        after = [pieces[part][3]]
    after = []
    for part in parts:
        total = weighted(total_kernel, lanes[part][0], *pieces[part], *after)
        if part == 0:
            one = intra(1, (0, cut), total)
            after = [one]
        befores.append([later(total, shift) for shift in range(1, groups)])
    zero_rest = intra(0, (cut, heads), total)
    after = [zero_rest]
    for part in parts:
        outs = weighted(functools.partial(carry_kernel, groups - 1), lanes[part], *pieces[part], *befores[part], *after)
        states.append(exchange(outs))
        if part == 0:
            one_rest = intra(1, (cut, heads), outs[0])
            after = [one_rest]
    for part in parts:
        siblings.append(swap(weighted(pair_kernel, talls[part], keeps[part], *states[part]), 1))
    intras = [zero, one, zero_rest, one_rest]
    mixed, squares = weighted(
        functools.partial(mix_kernel, cut), [array((rows, width)), array((rows, HD))], use, query, *intras,
        *[piece for pieces in states for piece in pieces], *gots, *siblings[:-1])
    attended = call(
        norm_kernel, array((rows, width), BF16), use, query, norm_gain[None, :], mixed, squares, siblings[-1],
        scratch=[pltpu.VMEM((rows, talls[-1].shape[0]), F32)])
    return attended[None]


def solution(mesh):
    placed = (
        P("sess", "ctx", None),
        P("sess", "ctx", None),
        P("sess", "ctx", None),
        P("sess", None),
        P(),
    )
    return jax.shard_map(
        functools.partial(shards, mesh.shape["ctx"]), mesh=mesh, in_specs=placed,
        out_specs=P("sess", "ctx", None), check_vma=False
    )
```

```python
import functools

import jax
import jax.numpy as jnp
from jax import lax
from jax.experimental import pallas as pl
from jax.experimental.pallas import tpu as pltpu
from jax.sharding import PartitionSpec as P

HD = 128
CHIPS = 4
QUARTERS = (0, 3, 2, 1)
FRONT = (((0, 1, 2, 3),), ((0, 1, 2, 3),))
BACK = (((0, 1, 2, 3),), ((0, 1, 2, 3),))
SPLIT = (1, 1)
SLOTS = {"start": [(0, (0, 16))], "between1": [(0, (16, 32))], "enter1": [(1, (0, 32))]}
F32 = jnp.float32
BF16 = jnp.bfloat16
HB = pl.BlockSpec(memory_space=pltpu.HBM)
SM = pl.BlockSpec(memory_space=pltpu.SMEM)
VM = pl.BlockSpec(memory_space=pltpu.VMEM)
PARAMS = pltpu.CompilerParams(vmem_limit_bytes=32 * 1024 * 1024)


def place():
    block = lax.axis_index("ctx")
    return block % 2, (block // 2) % CHIPS, block // (2 * CHIPS), block


def segment_at(starts, position):
    count = jnp.int32(0)
    for i in range(starts.shape[1]):
        count = count + (starts[0, i] <= position).astype(jnp.int32)
    return count


def same(starts, rows, late, early):
    one = segment_at(starts, (late + 1) * rows - 1)
    two = segment_at(starts, (early + 1) * rows - 1)
    return (one == two).astype(F32)


def segment_rows(starts, positions):
    count = jnp.zeros(positions.shape, jnp.int32)
    for i in range(starts.shape[1]):
        count = count + (starts[0, i] <= positions).astype(jnp.int32)
    return count


def tile(index):
    return slice(index * HD, (index + 1) * HD)


def sizes(width):
    quarter = width // HD // 2 // CHIPS
    return [quarter * share // sum(SPLIT) for share in SPLIT]


def part_steps(width, part, spots=range(CHIPS)):
    return [(part, QUARTERS[spot], j) for spot in spots for j in range(sizes(width)[part])]


def steps(width):
    return [
        (own, *step) for own in (True, False) for part in range(len(SPLIT)) for spots in BACK[part]
        for step in part_steps(width, part, spots)]


def found_in(groups, spot):
    return next((i, group.index(spot)) for i, group in enumerate(groups) if spot in group)


def column(width, core, chip, own, part, k, j):
    parts = sizes(width)
    quarter = sum(parts)
    half = core if own else 1 - core
    head = (half * CHIPS + lax.bitwise_xor(chip, k)) * quarter + sum(parts[:part]) + j
    return pl.ds(pl.multiple_of(head * HD, HD), HD)


def table_rows(groups):
    names = ["chip_mine", "chip_other", "pair_scale", "pair_add", "mix_scale", "mix_add"]
    names += [("total", k) for k in range(CHIPS)]
    names += [("carry", k, j) for k in range(CHIPS) for j in range(CHIPS)]
    names += [("enter", k) for k in range(CHIPS)]
    names += [("before", s) for s in range(groups - 1)]
    return {name: i for i, name in enumerate(names)}


def weights(starts, rows, groups):
    core, chip, group, block = place()
    same_ = functools.partial(same, starts, rows)
    mine, first = block // 2 * 2, group * 2 * CHIPS
    joined = same_(mine + 1, mine)
    after, mix = same_(block, block - 1), same_(block - 1, block - 2)
    found = {
        "chip_mine": jnp.where(core == 0, joined, 1.0),
        "chip_other": jnp.where(core == 0, 1.0, joined),
        "pair_scale": jnp.where(core == 0, after, 1.0),
        "pair_add": jnp.where(core == 0, 1.0, 0.0),
        "mix_scale": jnp.where(core == 0, 1.0, mix),
        "mix_add": jnp.where(core == 0, 0.0, 1.0),
    }
    for k in range(CHIPS):
        target = lax.bitwise_xor(chip, k)
        end = first + 2 * target - 1
        found["total", k] = same_(first + 7, first + 2 * target + 1)
        found["enter", k] = same_(end, first - 1)
        for j in range(CHIPS):
            source = lax.bitwise_xor(chip, j)
            found["carry", k, j] = jnp.where(source < target, same_(end, first + 2 * source + 1), 0.0)
    for s in range(groups - 1):
        end = first - 1 - s * 2 * CHIPS
        found["before", s] = jnp.where(end >= 0, same_(first - 1, end), 0.0)
    return found


def summarize(kept_ref, key_ref, value_ref, own, part, spots, out):
    core, chip, _, _ = place()
    width = key_ref.shape[1]
    kept = kept_ref[...]
    for i, step in enumerate(part_steps(width, part, spots)):
        at = column(width, core, chip, own, *step)
        out[tile(i), :] = lax.dot_general(
            key_ref[:, at] * kept, value_ref[:, at], (((0,), (0,)), ((), ())), preferred_element_type=F32)


def first_kernel(groups, starts_hbm, key_hbm, value_hbm, key_ref, value_ref, table_ref, kept_ref, allowed_ref, use_ref, *refs):
    *sends, starts, sems = refs
    copies = [
        pltpu.make_async_copy(source, target, sems.at[i])
        for i, (source, target) in enumerate(((starts_hbm, starts), (key_hbm, key_ref), (value_hbm, value_ref)))
    ]
    for copy in copies:
        copy.start()
    copies[0].wait()
    rows = key_ref.shape[0]
    begin = place()[3] * rows
    names = table_rows(groups)
    for name, weight in weights(starts, rows, groups).items():
        table_ref[names[name]:names[name] + 1, :] = jnp.full((1, HD), weight, F32)
    segments = segment_rows(starts, begin + lax.broadcasted_iota(jnp.int32, (rows, HD), 0))
    kept_ref[...] = (segments == segment_at(starts, begin + rows - 1)).astype(F32).astype(BF16)
    use_ref[...] = (segments == segment_at(starts, begin - 1)).astype(F32)
    late = begin + lax.broadcasted_iota(jnp.int32, (rows, rows), 0)
    early = begin + lax.broadcasted_iota(jnp.int32, (rows, rows), 1)
    allowed = (late >= early) & (segment_rows(starts, late) == segment_rows(starts, early))
    allowed_ref[...] = allowed.astype(F32)
    for copy in copies[1:]:
        copy.wait()
    for spots, send_ref in zip(FRONT[0], sends):
        summarize(kept_ref, key_ref, value_ref, False, 0, spots, send_ref)


def summary_kernel(what, kept_ref, key_ref, value_ref, *refs):
    for (own, part, spots), out in zip(what, refs[-len(what):]):
        summarize(kept_ref, key_ref, value_ref, own, part, spots, out)


def row(table_ref, groups, *name):
    at = table_rows(groups)[name if len(name) > 1 else name[0]]
    return table_ref[at:at + 1, :]


def chip_kernel(count, weight, keep_ref, got_ref, *refs):
    size = refs[-1].shape[0]
    for i, out in enumerate(refs[-count:]):
        at = slice(i * size, (i + 1) * size)
        out[...] = weight("chip_mine") * keep_ref[at, :] + weight("chip_other") * got_ref[at, :]


def total_kernel(weight, *refs):
    total = None
    for k, piece in zip(QUARTERS, refs[:CHIPS]):
        term = weight("total", k) * piece[...]
        total = term if total is None else total + term
    refs[-1][...] = total


def straight_kernel(shifts, weight, *refs):
    pieces, outs = refs[:CHIPS], refs[-CHIPS:]
    before = entered(weight, refs[CHIPS:CHIPS + shifts])
    for k, out in zip(QUARTERS, outs):
        state = weight("enter", k) * before
        for j, piece in zip(QUARTERS, pieces):
            if j != k:
                state = state + weight("carry", k, j) * piece[...]
        out[...] = state


def entered(weight, totals):
    before = None
    for s, total in enumerate(totals):
        term = weight("before", s) * total[...]
        before = term if before is None else before + term
    return before


def pair_kernel(part, spots, weight, *refs):
    keeps, pieces, out = refs[:len(FRONT[part])], refs[len(FRONT[part]):][:len(spots)], refs[-1]
    size = pieces[0].shape[0]
    for i, (spot, piece) in enumerate(zip(spots, pieces)):
        which, place_in = found_in(FRONT[part], spot)
        keep = keeps[which][place_in * size:(place_in + 1) * size, :]
        out[i * size:(i + 1) * size, :] = weight("pair_scale") * piece[...] + weight("pair_add") * keep


def intra_kernel(on, span, allowed_ref, query_ref, key_ref, value_ref, *refs):
    out_ref = refs[-1]
    core, chip, _, _ = place()
    width = query_ref.shape[1]

    def body():
        allowed = allowed_ref[...]
        for i, step in enumerate(steps(width)[slice(*span)]):
            at = column(width, core, chip, *step)
            scores = lax.dot_general(
                query_ref[:, at], key_ref[:, at], (((1,), (1,)), ((), ())), preferred_element_type=F32)
            out_ref[:, tile(i)] = jnp.dot(
                (scores * allowed).astype(BF16), value_ref[:, at], preferred_element_type=F32)

    if on is None:
        body()
    else:
        pl.when(core == on)(body)


def from_past(use, query_ref, step, state):
    core, chip, _, _ = place()
    at = column(query_ref.shape[1], core, chip, *step)
    return use * jnp.dot(query_ref[:, at], state.astype(BF16), preferred_element_type=F32)


def mix_kernel(sources, count, weight, use_ref, query_ref, gain_ref, *refs):
    parts = len(SPLIT)
    intras, refs = refs[:count], refs[count:]
    states = [refs[part * CHIPS:(part + 1) * CHIPS] for part in range(parts)]
    refs = refs[parts * CHIPS:]
    gots, siblings = [], []
    for part in range(parts):
        gots.append(refs[:len(FRONT[part])])
        refs = refs[len(FRONT[part]):]
    for part in range(parts):
        siblings.append(refs[:len(BACK[part])])
        refs = refs[len(siblings[part]):] if part < parts - 1 else refs
    mixed_ref, squares_ref = refs[-2:]
    core, chip, _, _ = place()
    rows, width = query_ref.shape
    use = use_ref[...]
    squares = jnp.zeros((rows, HD), F32)
    order = steps(width)
    first = len(order) - len(part_steps(width, parts - 1, BACK[-1][-1]))
    for i, step in enumerate(order):
        found = [intras[which][:, tile(at)] for which, at in sources[i]]
        both = found[0] if sources[i][0] == sources[i][1] else jnp.where(core == 0, *found)
        own, part, k, j = step
        size = sizes(width)[part]
        spot = QUARTERS.index(k)
        if own:
            which, at = found_in(FRONT[part], spot)
            state = weight("mix_scale") * states[part][spot][tile(j), :]
            state = state + weight("mix_add") * gots[part][which][tile(at * size + j), :]
        elif i < first:
            which, at = found_in(BACK[part], spot)
            state = siblings[part][which][tile(at * size + j), :]
        else:
            mixed_ref[:, tile(i)] = both
            continue
        both = both + from_past(use, query_ref, step, state)
        squares = squares + both * both
        mixed_ref[:, tile(i)] = both * gain_ref[:, column(width, core, chip, *step)]
    squares_ref[...] = squares


def norm_kernel(use_ref, query_ref, gain_ref, mixed_ref, squares_ref, sibling_ref, out_hbm, out_ref, sems):
    core, chip, _, _ = place()
    rows, width = query_ref.shape
    order = steps(width)
    first = len(order) - sibling_ref.shape[0] // HD
    use = use_ref[...]
    squares = squares_ref[...]
    late = []
    for i, step in enumerate(order[first:]):
        both = mixed_ref[:, tile(first + i)] + from_past(use, query_ref, step, sibling_ref[tile(i), :])
        squares = squares + both * both
        late.append(both * gain_ref[:, column(width, core, chip, *step)])
    mean = jnp.sum(squares, axis=-1, keepdims=True) * (1.0 / width)
    norm = jnp.broadcast_to(lax.rsqrt(mean + 1e-05), (rows, HD))
    for i, step in enumerate(order):
        both = mixed_ref[:, tile(i)] if i < first else late[i - first]
        out_ref[:, column(width, core, chip, *step)] = (both * norm).astype(BF16)
    copies = []
    for i in range(sems.shape[0]):
        at = slice(i * rows // sems.shape[0], (i + 1) * rows // sems.shape[0])
        copies.append(pltpu.make_async_copy(out_ref.at[at, :], out_hbm.at[at, :], sems.at[i]))
        copies[-1].start()
    for copy in copies:
        copy.wait()


def in_hbm(array):
    return pltpu.with_memory_space_constraint(array, pltpu.HBM)


def array(shape, dtype=F32):
    return jax.ShapeDtypeStruct(shape, dtype)


def shards(count, query_rows, key_rows, value_rows, seg_starts, norm_gain):
    query, key, value = query_rows[0], key_rows[0], value_rows[0]
    rows, width = query.shape
    groups = count // (2 * CHIPS)
    parts = range(len(SPLIT))
    heads = len(steps(width))
    lanes = [array((size * HD, HD)) for size in sizes(width)]

    def tall(part, spots):
        return array((len(part_steps(width, part, spots)) * HD, HD))

    def call(kernel, outs, *args, scratch=()):
        return pl.pallas_call(
            kernel, out_shape=outs, in_specs=[VM] * len(args), out_specs=jax.tree.map(lambda _: VM, outs),
            scratch_shapes=scratch, compiler_params=PARAMS,
        )(*args)

    def weighted(kernel, outs, *args):
        def body(table_ref, *refs):
            return kernel(functools.partial(row, table_ref, groups), *refs)

        return call(body, outs, table, *args)

    def swap(what, bits):
        return lax.ppermute(what, "ctx", [(i, i ^ bits) for i in range(count)])

    def later(what, shift):
        return lax.ppermute(what, "ctx", [(i, (i + shift * 2 * CHIPS) % count) for i in range(count)])

    def intra(on, span, *after):
        out = array((rows, (span[1] - span[0]) * HD))
        return call(functools.partial(intra_kernel, on, span), out, allowed, query, key, value, *after)

    def summary(what, *after):
        outs = [tall(*step[1:]) for step in what]
        return call(functools.partial(summary_kernel, what), outs, kept, key, value, *after)

    key, value, table, kept, allowed, use, *sends = pl.pallas_call(
        functools.partial(first_kernel, groups),
        out_shape=[array((rows, width), BF16)] * 2 + [
            array((-(-len(table_rows(groups)) // 8) * 8, HD)), array((rows, HD), BF16), array((rows, rows)),
            array((rows, HD))] + [tall(0, spots) for spots in FRONT[0]],
        in_specs=[HB] * 3, out_specs=[VM] * (6 + len(FRONT[0])),
        scratch_shapes=[pltpu.SMEM(seg_starts.shape, jnp.int32), pltpu.SemaphoreType.DMA((3,))],
        compiler_params=PARAMS,
    )(in_hbm(seg_starts), in_hbm(key), in_hbm(value))
    gots, keeps = [], []
    for part in parts:
        gots.append([swap(send, 1) for send in sends])
        keep = [(True, part, spots) for spots in FRONT[part]]
        send = [(False, part + 1, spots) for spots in FRONT[part + 1]] if part + 1 < len(SPLIT) else []
        outs = summary(keep + send)
        keeps.append(outs[:len(keep)])
        sends = outs[len(keep):]
    done = [[None] * heads, [None] * heads]
    intras = []

    def inside(slot, *after):
        new = []
        for on, span in SLOTS.get(slot, ()):
            span = tuple(heads * at // 32 for at in span)
            for core in range(2) if on is None else (on,):
                done[core][slice(*span)] = [(len(intras), i) for i in range(span[1] - span[0])]
            intras.append(intra(on, span, *after))
            new.append(intras[-1])
        return new

    chips, totals, states, siblings = [{} for _ in range(4)]

    def begin(part, *after):
        own = {}
        for spots, keep, got in zip(FRONT[part], keeps[part], gots[part]):
            outs = weighted(
                functools.partial(chip_kernel, len(spots)), [lanes[part]] * len(spots), keep, got, *after)
            own.update(zip(spots, outs))
        chips[part] = {spot: swap(own[spot], 2 * QUARTERS[spot]) if QUARTERS[spot] else own[spot] for spot in own}
        return chips[part]

    def between(part, *after):
        total = weighted(total_kernel, lanes[part], *[chips[part][spot] for spot in range(CHIPS)], *after)
        totals[part] = [later(total, shift) for shift in range(1, groups)]
        return [total]

    def enter(part, *after):
        outs = weighted(
            functools.partial(straight_kernel, groups - 1), [lanes[part]] * CHIPS,
            *[chips[part][spot] for spot in range(CHIPS)], *totals[part], *after)
        states[part] = [swap(out, 2 * k) if k else out for out, k in zip(outs, QUARTERS)]
        return [outs[0]]

    def share(part, *after):
        siblings[part] = []
        for spots in BACK[part]:
            siblings[part].append(swap(weighted(
                functools.partial(pair_kernel, part, spots), tall(part, spots), *keeps[part],
                *[states[part][spot] for spot in spots], *after), 1))
        return siblings[part][:1]

    a = begin(0, *inside("start", keeps[0][0]))
    b = begin(1, a[1])
    a = between(0, *inside("begin", b[0]))
    b = between(1, *inside("between", a[0]))
    a = enter(0, *inside("between1", b[0]))
    b = enter(1, *inside("enter", a[0]))
    a = share(0, *inside("enter1", b[0]))
    b = share(1, *inside("share", a[0]))
    siblings, states = [siblings[part] for part in parts], [states[part] for part in parts]
    gain = norm_gain[None, :]
    mixed, squares = weighted(
        functools.partial(mix_kernel, list(zip(*done)), len(intras)), [array((rows, width)), array((rows, HD))], use, query, gain,
        *intras, *[piece for state in states for piece in state], *[got for group in gots for got in group],
        *[sibling for group in siblings for sibling in group][:-1])
    attended = pl.pallas_call(
        norm_kernel, out_shape=array((rows, width), BF16), in_specs=[VM] * 6, out_specs=HB,
        scratch_shapes=[pltpu.VMEM((rows, width), BF16), pltpu.SemaphoreType.DMA((2,))], compiler_params=PARAMS,
    )(use, query, gain, mixed, squares, siblings[-1][-1])
    return attended[None]


def solution(mesh):
    placed = (
        P("sess", "ctx", None),
        P("sess", "ctx", None),
        P("sess", "ctx", None),
        P("sess", None),
        P(),
    )
    return jax.shard_map(
        functools.partial(shards, mesh.shape["ctx"]), mesh=mesh, in_specs=placed,
        out_specs=P("sess", "ctx", None), check_vma=False
    )
```

```python
import functools

import jax
import jax.numpy as jnp
from jax import lax
from jax.experimental import pallas as pl
from jax.experimental.pallas import tpu as pltpu
from jax.sharding import PartitionSpec as P

HD = 128
CHIPS = 4
QUARTERS = (0, 3, 2, 1)
FRONT = (((0, 1, 2, 3),), ((0, 1, 2, 3),))
BACK = (((0, 1, 2, 3),), ((0, 1, 2, 3),))
SPLIT = (1, 1)
SLOTS = {"start": [(0, (0, 16))], "between1": [(0, (16, 32))], "enter1": [(1, (0, 32))]}
F32 = jnp.float32
BF16 = jnp.bfloat16
HB = pl.BlockSpec(memory_space=pltpu.HBM)
SM = pl.BlockSpec(memory_space=pltpu.SMEM)
VM = pl.BlockSpec(memory_space=pltpu.VMEM)
PARAMS = pltpu.CompilerParams(vmem_limit_bytes=32 * 1024 * 1024)


def place():
    block = lax.axis_index("ctx")
    return block % 2, (block // 2) % CHIPS, block // (2 * CHIPS), block


def segment_at(starts, position):
    count = jnp.int32(0)
    for i in range(starts.shape[1]):
        count = count + (starts[0, i] <= position).astype(jnp.int32)
    return count


def same(starts, rows, late, early):
    one = segment_at(starts, (late + 1) * rows - 1)
    two = segment_at(starts, (early + 1) * rows - 1)
    return (one == two).astype(F32)


def segment_rows(starts, positions):
    count = jnp.zeros(positions.shape, jnp.int32)
    for i in range(starts.shape[1]):
        count = count + (starts[0, i] <= positions).astype(jnp.int32)
    return count


def tile(index):
    return slice(index * HD, (index + 1) * HD)


def sizes(width):
    quarter = width // HD // 2 // CHIPS
    return [quarter * share // sum(SPLIT) for share in SPLIT]


def part_steps(width, part, spots=range(CHIPS)):
    return [(part, QUARTERS[spot], j) for spot in spots for j in range(sizes(width)[part])]


def steps(width):
    return [
        (own, *step) for own in (True, False) for part in range(len(SPLIT)) for spots in BACK[part]
        for step in part_steps(width, part, spots)]


def found_in(groups, spot):
    return next((i, group.index(spot)) for i, group in enumerate(groups) if spot in group)


def column(width, core, chip, own, part, k, j):
    parts = sizes(width)
    quarter = sum(parts)
    half = core if own else 1 - core
    head = (half * CHIPS + lax.bitwise_xor(chip, k)) * quarter + sum(parts[:part]) + j
    return pl.ds(pl.multiple_of(head * HD, HD), HD)


def table_rows(groups):
    names = ["chip_mine", "chip_other", "pair_scale", "pair_add", "mix_scale", "mix_add"]
    names += [("total", k) for k in range(CHIPS)]
    names += [("carry", k, j) for k in range(CHIPS) for j in range(CHIPS)]
    names += [("enter", k) for k in range(CHIPS)]
    names += [("before", s) for s in range(groups - 1)]
    return {name: i for i, name in enumerate(names)}


def weights(starts, rows, groups):
    core, chip, group, block = place()
    same_ = functools.partial(same, starts, rows)
    mine, first = block // 2 * 2, group * 2 * CHIPS
    joined = same_(mine + 1, mine)
    after, mix = same_(block, block - 1), same_(block - 1, block - 2)
    found = {
        "chip_mine": jnp.where(core == 0, joined, 1.0),
        "chip_other": jnp.where(core == 0, 1.0, joined),
        "pair_scale": jnp.where(core == 0, after, 1.0),
        "pair_add": jnp.where(core == 0, 1.0, 0.0),
        "mix_scale": jnp.where(core == 0, 1.0, mix),
        "mix_add": jnp.where(core == 0, 0.0, 1.0),
    }
    for k in range(CHIPS):
        target = lax.bitwise_xor(chip, k)
        end = first + 2 * target - 1
        found["total", k] = same_(first + 7, first + 2 * target + 1)
        found["enter", k] = same_(end, first - 1)
        for j in range(CHIPS):
            source = lax.bitwise_xor(chip, j)
            found["carry", k, j] = jnp.where(source < target, same_(end, first + 2 * source + 1), 0.0)
    for s in range(groups - 1):
        end = first - 1 - s * 2 * CHIPS
        found["before", s] = jnp.where(end >= 0, same_(first - 1, end), 0.0)
    return found


def summarize(kept_ref, key_ref, value_ref, own, part, spots, out):
    core, chip, _, _ = place()
    width = key_ref.shape[1]
    kept = kept_ref[...]
    for i, step in enumerate(part_steps(width, part, spots)):
        at = column(width, core, chip, own, *step)
        out[tile(i), :] = lax.dot_general(
            key_ref[:, at] * kept, value_ref[:, at], (((0,), (0,)), ((), ())), preferred_element_type=F32)


def first_kernel(groups, starts_hbm, key_hbm, value_hbm, key_ref, value_ref, table_ref, kept_ref, allowed_ref, use_ref, *refs):
    *sends, starts, sems = refs
    copies = [
        pltpu.make_async_copy(source, target, sems.at[i])
        for i, (source, target) in enumerate(((starts_hbm, starts), (key_hbm, key_ref), (value_hbm, value_ref)))
    ]
    for copy in copies:
        copy.start()
    copies[0].wait()
    rows = key_ref.shape[0]
    begin = place()[3] * rows
    names = table_rows(groups)
    for name, weight in weights(starts, rows, groups).items():
        table_ref[names[name]:names[name] + 1, :] = jnp.full((1, HD), weight, F32)
    segments = segment_rows(starts, begin + lax.broadcasted_iota(jnp.int32, (rows, HD), 0))
    kept_ref[...] = (segments == segment_at(starts, begin + rows - 1)).astype(F32).astype(BF16)
    use_ref[...] = (segments == segment_at(starts, begin - 1)).astype(F32)
    late = begin + lax.broadcasted_iota(jnp.int32, (rows, rows), 0)
    early = begin + lax.broadcasted_iota(jnp.int32, (rows, rows), 1)
    allowed = (late >= early) & (segment_rows(starts, late) == segment_rows(starts, early))
    allowed_ref[...] = allowed.astype(F32)
    for copy in copies[1:]:
        copy.wait()
    for spots, send_ref in zip(FRONT[0], sends):
        summarize(kept_ref, key_ref, value_ref, False, 0, spots, send_ref)


def summary_kernel(what, kept_ref, key_ref, value_ref, *refs):
    for (own, part, spots), out in zip(what, refs[-len(what):]):
        summarize(kept_ref, key_ref, value_ref, own, part, spots, out)


def row(table_ref, groups, *name):
    at = table_rows(groups)[name if len(name) > 1 else name[0]]
    return table_ref[at:at + 1, :]


def chip_kernel(count, weight, keep_ref, got_ref, *refs):
    size = refs[-1].shape[0]
    for i, out in enumerate(refs[-count:]):
        at = slice(i * size, (i + 1) * size)
        out[...] = weight("chip_mine") * keep_ref[at, :] + weight("chip_other") * got_ref[at, :]


def total_kernel(weight, *refs):
    total = None
    for k, piece in zip(QUARTERS, refs[:CHIPS]):
        term = weight("total", k) * piece[...]
        total = term if total is None else total + term
    refs[-1][...] = total


def straight_kernel(shifts, weight, *refs):
    pieces, outs = refs[:CHIPS], refs[-CHIPS:]
    before = entered(weight, refs[CHIPS:CHIPS + shifts])
    for k, out in zip(QUARTERS, outs):
        state = weight("enter", k) * before
        for j, piece in zip(QUARTERS, pieces):
            if j != k:
                state = state + weight("carry", k, j) * piece[...]
        out[...] = state


def entered(weight, totals):
    before = None
    for s, total in enumerate(totals):
        term = weight("before", s) * total[...]
        before = term if before is None else before + term
    return before


def query_kernel(query_ref, *refs):
    core, chip, _, _ = place()
    width = query_ref.shape[1]
    order = steps(width)
    half = len(order) // 2
    for i, step in enumerate(order[half:]):
        refs[-1][:, tile(i)] = query_ref[:, column(width, core, chip, *step)].astype(F32)


def pair_kernel(part, spots, weight, *refs):
    keeps, pieces = refs[:len(FRONT[part])], refs[len(FRONT[part]):][:len(spots)]
    query_ref, out = refs[len(keeps) + len(spots)], refs[-1]
    width = 2 * query_ref.shape[1]
    order = steps(width)
    size = pieces[0].shape[0]
    for i, (spot, piece) in enumerate(zip(spots, pieces)):
        which, place_in = found_in(FRONT[part], spot)
        keep = keeps[which][place_in * size:(place_in + 1) * size, :]
        state = (weight("pair_scale") * piece[...] + weight("pair_add") * keep).astype(BF16)
        for j in range(size // HD):
            query = query_ref[:, tile(order.index((True, part, QUARTERS[spot], j)))].astype(BF16)
            out[:, tile(i * (size // HD) + j)] = jnp.dot(query, state[tile(j), :], preferred_element_type=F32)


def intra_kernel(on, span, allowed_ref, query_ref, key_ref, value_ref, *refs):
    out_ref = refs[-1]
    core, chip, _, _ = place()
    width = query_ref.shape[1]

    def body():
        allowed = allowed_ref[...]
        for i, step in enumerate(steps(width)[slice(*span)]):
            at = column(width, core, chip, *step)
            scores = lax.dot_general(
                query_ref[:, at], key_ref[:, at], (((1,), (1,)), ((), ())), preferred_element_type=F32)
            out_ref[:, tile(i)] = jnp.dot(
                (scores * allowed).astype(BF16), value_ref[:, at], preferred_element_type=F32)

    if on is None:
        body()
    else:
        pl.when(core == on)(body)


def from_past(use, query_ref, step, state):
    core, chip, _, _ = place()
    at = column(query_ref.shape[1], core, chip, *step)
    return use * jnp.dot(query_ref[:, at], state.astype(BF16), preferred_element_type=F32)


def mix_kernel(sources, count, weight, use_ref, query_ref, gain_ref, *refs):
    parts = len(SPLIT)
    intras, refs = refs[:count], refs[count:]
    states = [refs[part * CHIPS:(part + 1) * CHIPS] for part in range(parts)]
    refs = refs[parts * CHIPS:]
    gots, siblings = [], []
    for part in range(parts):
        gots.append(refs[:len(FRONT[part])])
        refs = refs[len(FRONT[part]):]
    for part in range(parts):
        siblings.append(refs[:len(BACK[part])])
        refs = refs[len(siblings[part]):] if part < parts - 1 else refs
    mixed_ref, squares_ref = refs[-2:]
    core, chip, _, _ = place()
    rows, width = query_ref.shape
    use = use_ref[...]
    squares = jnp.zeros((rows, HD), F32)
    order = steps(width)
    first = len(order) - len(part_steps(width, parts - 1, BACK[-1][-1]))
    for i, step in enumerate(order):
        found = [intras[which][:, tile(at)] for which, at in sources[i]]
        both = found[0] if sources[i][0] == sources[i][1] else jnp.where(core == 0, *found)
        own, part, k, j = step
        size = sizes(width)[part]
        spot = QUARTERS.index(k)
        if own:
            which, at = found_in(FRONT[part], spot)
            state = weight("mix_scale") * states[part][spot][tile(j), :]
            state = state + weight("mix_add") * gots[part][which][tile(at * size + j), :]
            past = from_past(use, query_ref, step, state)
        elif i < first:
            which, at = found_in(BACK[part], spot)
            past = use * siblings[part][which][:, tile(at * size + j)]
        else:
            mixed_ref[:, tile(i)] = both
            continue
        both = both + past
        squares = squares + both * both
        mixed_ref[:, tile(i)] = both * gain_ref[:, column(width, core, chip, *step)]
    squares_ref[...] = squares


def norm_kernel(use_ref, gain_ref, mixed_ref, squares_ref, sibling_ref, out_hbm, out_ref, sems):
    core, chip, _, _ = place()
    rows, width = out_ref.shape
    order = steps(width)
    first = len(order) - sibling_ref.shape[1] // HD
    use = use_ref[...]
    squares = squares_ref[...]
    late = []
    for i, step in enumerate(order[first:]):
        both = mixed_ref[:, tile(first + i)] + use * sibling_ref[:, tile(i)]
        squares = squares + both * both
        late.append(both * gain_ref[:, column(width, core, chip, *step)])
    mean = jnp.sum(squares, axis=-1, keepdims=True) * (1.0 / width)
    norm = jnp.broadcast_to(lax.rsqrt(mean + 1e-05), (rows, HD))
    copies = []
    number = sems.shape[0]
    for part in range(number):
        at = slice(part * rows // number, (part + 1) * rows // number)
        for i, step in enumerate(order):
            both = mixed_ref[at, tile(i)] if i < first else late[i - first][at, :]
            out_ref[at, column(width, core, chip, *step)] = (both * norm[at, :]).astype(BF16)
        copies.append(pltpu.make_async_copy(out_ref.at[at, :], out_hbm.at[at, :], sems.at[part]))
        copies[-1].start()
    for copy in copies:
        copy.wait()


def in_hbm(array):
    return pltpu.with_memory_space_constraint(array, pltpu.HBM)


def array(shape, dtype=F32):
    return jax.ShapeDtypeStruct(shape, dtype)


def shards(count, query_rows, key_rows, value_rows, seg_starts, norm_gain):
    query, key, value = query_rows[0], key_rows[0], value_rows[0]
    rows, width = query.shape
    groups = count // (2 * CHIPS)
    parts = range(len(SPLIT))
    heads = len(steps(width))
    lanes = [array((size * HD, HD)) for size in sizes(width)]

    def tall(part, spots):
        return array((len(part_steps(width, part, spots)) * HD, HD))

    def call(kernel, outs, *args, scratch=()):
        return pl.pallas_call(
            kernel, out_shape=outs, in_specs=[VM] * len(args), out_specs=jax.tree.map(lambda _: VM, outs),
            scratch_shapes=scratch, compiler_params=PARAMS,
        )(*args)

    def weighted(kernel, outs, *args):
        def body(table_ref, *refs):
            return kernel(functools.partial(row, table_ref, groups), *refs)

        return call(body, outs, table, *args)

    def swap(what, bits):
        return lax.ppermute(what, "ctx", [(i, i ^ bits) for i in range(count)])

    def later(what, shift):
        return lax.ppermute(what, "ctx", [(i, (i + shift * 2 * CHIPS) % count) for i in range(count)])

    def intra(on, span, *after):
        out = array((rows, (span[1] - span[0]) * HD))
        return call(functools.partial(intra_kernel, on, span), out, allowed, query, key, value, *after)

    def summary(what, *after):
        outs = [tall(*step[1:]) for step in what]
        return call(functools.partial(summary_kernel, what), outs, kept, key, value, *after)

    key, value, table, kept, allowed, use, *sends = pl.pallas_call(
        functools.partial(first_kernel, groups),
        out_shape=[array((rows, width), BF16)] * 2 + [
            array((-(-len(table_rows(groups)) // 8) * 8, HD)), array((rows, HD), BF16), array((rows, rows)),
            array((rows, HD))] + [tall(0, spots) for spots in FRONT[0]],
        in_specs=[HB] * 3, out_specs=[VM] * (6 + len(FRONT[0])),
        scratch_shapes=[pltpu.SMEM(seg_starts.shape, jnp.int32), pltpu.SemaphoreType.DMA((3,))],
        compiler_params=PARAMS,
    )(in_hbm(seg_starts), in_hbm(key), in_hbm(value))
    gots, keeps = [], []
    for part in parts:
        gots.append([swap(send, 1) for send in sends])
        keep = [(True, part, spots) for spots in FRONT[part]]
        send = [(False, part + 1, spots) for spots in FRONT[part + 1]] if part + 1 < len(SPLIT) else []
        outs = summary(keep + send)
        keeps.append(outs[:len(keep)])
        sends = outs[len(keep):]
    done = [[None] * heads, [None] * heads]
    intras = []

    def inside(slot, *after):
        new = []
        for on, span in SLOTS.get(slot, ()):
            span = tuple(heads * at // 32 for at in span)
            for core in range(2) if on is None else (on,):
                done[core][slice(*span)] = [(len(intras), i) for i in range(span[1] - span[0])]
            intras.append(intra(on, span, *after))
            new.append(intras[-1])
        return new

    chips, totals, states, siblings = [{} for _ in range(4)]

    def begin(part, *after):
        own = {}
        for spots, keep, got in zip(FRONT[part], keeps[part], gots[part]):
            outs = weighted(
                functools.partial(chip_kernel, len(spots)), [lanes[part]] * len(spots), keep, got, *after)
            own.update(zip(spots, outs))
        chips[part] = {spot: swap(own[spot], 2 * QUARTERS[spot]) if QUARTERS[spot] else own[spot] for spot in own}
        return chips[part]

    def between(part, *after):
        total = weighted(total_kernel, lanes[part], *[chips[part][spot] for spot in range(CHIPS)], *after)
        totals[part] = [later(total, shift) for shift in range(1, groups)]
        return [total]

    def enter(part, *after):
        outs = weighted(
            functools.partial(straight_kernel, groups - 1), [lanes[part]] * CHIPS,
            *[chips[part][spot] for spot in range(CHIPS)], *totals[part], *after)
        states[part] = [swap(out, 2 * k) if k else out for out, k in zip(outs, QUARTERS)]
        return [outs[0]]

    def share(part, *after):
        siblings[part] = []
        for spots in BACK[part]:
            siblings[part].append(swap(weighted(
                functools.partial(pair_kernel, part, spots), array((rows, tall(part, spots).shape[0])), *keeps[part],
                *[states[part][spot] for spot in spots], asked, *after), 1))
        return siblings[part][:1]

    asked = swap(call(query_kernel, array((rows, width // 2)), query), 1)
    a = begin(0, *inside("start", keeps[0][0]))
    b = begin(1, a[1], asked)
    a = between(0, *inside("begin", b[0]))
    b = between(1, *inside("between", a[0]))
    a = enter(0, *inside("between1", b[0]))
    b = enter(1, *inside("enter", a[0]))
    a = share(0, *inside("enter1", b[0]))
    b = share(1, *inside("share", a[0]))
    siblings, states = [siblings[part] for part in parts], [states[part] for part in parts]
    gain = norm_gain[None, :]
    mixed, squares = weighted(
        functools.partial(mix_kernel, list(zip(*done)), len(intras)), [array((rows, width)), array((rows, HD))], use, query, gain,
        *intras, *[piece for state in states for piece in state], *[got for group in gots for got in group],
        *[sibling for group in siblings for sibling in group][:-1])
    attended = pl.pallas_call(
        norm_kernel, out_shape=array((rows, width), BF16), in_specs=[VM] * 5, out_specs=HB,
        scratch_shapes=[pltpu.VMEM((rows, width), BF16), pltpu.SemaphoreType.DMA((2,))], compiler_params=PARAMS,
    )(use, gain, mixed, squares, siblings[-1][-1])
    return attended[None]


def solution(mesh):
    placed = (
        P("sess", "ctx", None),
        P("sess", "ctx", None),
        P("sess", "ctx", None),
        P("sess", None),
        P(),
    )
    return jax.shard_map(
        functools.partial(shards, mesh.shape["ctx"]), mesh=mesh, in_specs=placed,
        out_specs=P("sess", "ctx", None), check_vma=False
    )
```

```python
import functools

import jax
import jax.numpy as jnp
from jax import lax
from jax.experimental import pallas as pl
from jax.experimental.pallas import tpu as pltpu
from jax.sharding import PartitionSpec as P

HD = 128
CHIPS = 4
QUARTERS = (0, 3, 2, 1)
FRONT = (((0, 1, 2, 3),), ((0, 1, 2, 3),))
BACK = (((0, 1, 2, 3),), ((0, 1, 2, 3),))
SPLIT = (1, 1)
SLOTS = {'start': [(0, (0, 16))], 'enter1': [(0, (16, 32)), (1, (0, 32))]}
F32 = jnp.float32
BF16 = jnp.bfloat16
HB = pl.BlockSpec(memory_space=pltpu.HBM)
SM = pl.BlockSpec(memory_space=pltpu.SMEM)
VM = pl.BlockSpec(memory_space=pltpu.VMEM)
PARAMS = pltpu.CompilerParams(vmem_limit_bytes=32 * 1024 * 1024)


def place():
    block = lax.axis_index("ctx")
    return block % 2, (block // 2) % CHIPS, block // (2 * CHIPS), block


def segment_at(starts, position):
    count = jnp.int32(0)
    for i in range(starts.shape[1]):
        count = count + (starts[0, i] <= position).astype(jnp.int32)
    return count


def same(starts, rows, late, early):
    one = segment_at(starts, (late + 1) * rows - 1)
    two = segment_at(starts, (early + 1) * rows - 1)
    return (one == two).astype(F32)


def segment_rows(starts, positions):
    count = jnp.zeros(positions.shape, jnp.int32)
    for i in range(starts.shape[1]):
        count = count + (starts[0, i] <= positions).astype(jnp.int32)
    return count


def tile(index):
    return slice(index * HD, (index + 1) * HD)


def sizes(width):
    quarter = width // HD // 2 // CHIPS
    return [quarter * share // sum(SPLIT) for share in SPLIT]


def part_steps(width, part, spots=range(CHIPS)):
    return [(part, QUARTERS[spot], j) for spot in spots for j in range(sizes(width)[part])]


def steps(width):
    return [
        (own, *step) for own in (True, False) for part in range(len(SPLIT)) for spots in BACK[part]
        for step in part_steps(width, part, spots)]


def found_in(groups, spot):
    return next((i, group.index(spot)) for i, group in enumerate(groups) if spot in group)


def column(width, core, chip, own, part, k, j):
    parts = sizes(width)
    quarter = sum(parts)
    half = core if own else 1 - core
    head = (half * CHIPS + lax.bitwise_xor(chip, k)) * quarter + sum(parts[:part]) + j
    return pl.ds(pl.multiple_of(head * HD, HD), HD)


def table_rows(groups):
    names = ["chip_mine", "chip_other", "pair_scale", "pair_add", "mix_scale", "mix_add"]
    names += [("total", k) for k in range(CHIPS)]
    names += [("carry", k, j) for k in range(CHIPS) for j in range(CHIPS)]
    names += [("enter", k) for k in range(CHIPS)]
    names += [("before", s) for s in range(groups - 1)]
    return {name: i for i, name in enumerate(names)}


def weights(starts, rows, groups):
    core, chip, group, block = place()
    same_ = functools.partial(same, starts, rows)
    mine, first = block // 2 * 2, group * 2 * CHIPS
    joined = same_(mine + 1, mine)
    after, mix = same_(block, block - 1), same_(block - 1, block - 2)
    found = {
        "chip_mine": jnp.where(core == 0, joined, 1.0),
        "chip_other": jnp.where(core == 0, 1.0, joined),
        "pair_scale": jnp.where(core == 0, after, 1.0),
        "pair_add": jnp.where(core == 0, 1.0, 0.0),
        "mix_scale": jnp.where(core == 0, 1.0, mix),
        "mix_add": jnp.where(core == 0, 0.0, 1.0),
    }
    for k in range(CHIPS):
        target = lax.bitwise_xor(chip, k)
        end = first + 2 * target - 1
        found["total", k] = same_(first + 7, first + 2 * target + 1)
        found["enter", k] = same_(end, first - 1)
        for j in range(CHIPS):
            source = lax.bitwise_xor(chip, j)
            found["carry", k, j] = jnp.where(source < target, same_(end, first + 2 * source + 1), 0.0)
    for s in range(groups - 1):
        end = first - 1 - s * 2 * CHIPS
        found["before", s] = jnp.where(end >= 0, same_(first - 1, end), 0.0)
    return found


def summarize(kept_ref, key_ref, value_ref, own, part, spots, out):
    core, chip, _, _ = place()
    width = key_ref.shape[1]
    kept = kept_ref[...]
    for i, step in enumerate(part_steps(width, part, spots)):
        at = column(width, core, chip, own, *step)
        out[tile(i), :] = lax.dot_general(
            key_ref[:, at] * kept, value_ref[:, at], (((0,), (0,)), ((), ())), preferred_element_type=F32)


def first_kernel(groups, starts_hbm, key_hbm, value_hbm, key_ref, value_ref, table_ref, kept_ref, allowed_ref, use_ref, *refs):
    *sends, starts, sems = refs
    copies = [
        pltpu.make_async_copy(source, target, sems.at[i])
        for i, (source, target) in enumerate(((starts_hbm, starts), (key_hbm, key_ref), (value_hbm, value_ref)))
    ]
    for copy in copies:
        copy.start()
    copies[0].wait()
    rows = key_ref.shape[0]
    begin = place()[3] * rows
    names = table_rows(groups)
    for name, weight in weights(starts, rows, groups).items():
        table_ref[names[name]:names[name] + 1, :] = jnp.full((1, HD), weight, F32)
    segments = segment_rows(starts, begin + lax.broadcasted_iota(jnp.int32, (rows, HD), 0))
    kept_ref[...] = (segments == segment_at(starts, begin + rows - 1)).astype(F32).astype(BF16)
    use_ref[...] = (segments == segment_at(starts, begin - 1)).astype(F32)
    late = begin + lax.broadcasted_iota(jnp.int32, (rows, rows), 0)
    early = begin + lax.broadcasted_iota(jnp.int32, (rows, rows), 1)
    allowed = (late >= early) & (segment_rows(starts, late) == segment_rows(starts, early))
    allowed_ref[...] = allowed.astype(F32)
    for copy in copies[1:]:
        copy.wait()
    for spots, send_ref in zip(FRONT[0], sends):
        summarize(kept_ref, key_ref, value_ref, False, 0, spots, send_ref)


def summary_kernel(what, kept_ref, key_ref, value_ref, *refs):
    for (own, part, spots), out in zip(what, refs[-len(what):]):
        summarize(kept_ref, key_ref, value_ref, own, part, spots, out)


def row(table_ref, groups, *name):
    at = table_rows(groups)[name if len(name) > 1 else name[0]]
    return table_ref[at:at + 1, :]


def chip_kernel(count, weight, keep_ref, got_ref, *refs):
    size = refs[-1].shape[0]
    for i, out in enumerate(refs[-count:]):
        at = slice(i * size, (i + 1) * size)
        out[...] = weight("chip_mine") * keep_ref[at, :] + weight("chip_other") * got_ref[at, :]


def total_kernel(weight, *refs):
    total = None
    for k, piece in zip(QUARTERS, refs[:CHIPS]):
        term = weight("total", k) * piece[...]
        total = term if total is None else total + term
    refs[-1][...] = total


def straight_kernel(shifts, weight, *refs):
    pieces, outs = refs[:CHIPS], refs[-CHIPS:]
    before = entered(weight, refs[CHIPS:CHIPS + shifts])
    for k, out in zip(QUARTERS, outs):
        state = weight("enter", k) * before
        for j, piece in zip(QUARTERS, pieces):
            if j != k:
                state = state + weight("carry", k, j) * piece[...]
        out[...] = state


def entered(weight, totals):
    before = None
    for s, total in enumerate(totals):
        term = weight("before", s) * total[...]
        before = term if before is None else before + term
    return before


def query_kernel(query_ref, *refs):
    core, chip, _, _ = place()
    width = query_ref.shape[1]
    order = steps(width)
    half = len(order) // 2
    for i, step in enumerate(order[half:]):
        refs[-1][:, tile(i)] = query_ref[:, column(width, core, chip, *step)].astype(F32)


def pair_kernel(part, spots, weight, *refs):
    keeps, pieces = refs[:len(FRONT[part])], refs[len(FRONT[part]):][:len(spots)]
    query_ref, out = refs[len(keeps) + len(spots)], refs[-1]
    width = 2 * query_ref.shape[1]
    order = steps(width)
    size = pieces[0].shape[0]
    for i, (spot, piece) in enumerate(zip(spots, pieces)):
        which, place_in = found_in(FRONT[part], spot)
        keep = keeps[which][place_in * size:(place_in + 1) * size, :]
        state = (weight("pair_scale") * piece[...] + weight("pair_add") * keep).astype(BF16)
        for j in range(size // HD):
            query = query_ref[:, tile(order.index((True, part, QUARTERS[spot], j)))].astype(BF16)
            out[:, tile(i * (size // HD) + j)] = jnp.dot(query, state[tile(j), :], preferred_element_type=F32)


def intra_kernel(on, span, allowed_ref, query_ref, key_ref, value_ref, *refs):
    out_ref = refs[-1]
    core, chip, _, _ = place()
    width = query_ref.shape[1]

    def body():
        allowed = allowed_ref[...]
        for i, step in enumerate(steps(width)[slice(*span)]):
            at = column(width, core, chip, *step)
            scores = lax.dot_general(
                query_ref[:, at], key_ref[:, at], (((1,), (1,)), ((), ())), preferred_element_type=F32)
            out_ref[:, tile(i)] = jnp.dot(
                (scores * allowed).astype(BF16), value_ref[:, at], preferred_element_type=F32)

    if on is None:
        body()
    else:
        pl.when(core == on)(body)


def from_past(use, query_ref, step, state):
    core, chip, _, _ = place()
    at = column(query_ref.shape[1], core, chip, *step)
    return use * jnp.dot(query_ref[:, at], state.astype(BF16), preferred_element_type=F32)


def mix_kernel(sources, count, weight, use_ref, query_ref, gain_ref, *refs):
    parts = len(SPLIT)
    intras, refs = refs[:count], refs[count:]
    states = [refs[part * CHIPS:(part + 1) * CHIPS] for part in range(parts)]
    refs = refs[parts * CHIPS:]
    gots, siblings = [], []
    for part in range(parts):
        gots.append(refs[:len(FRONT[part])])
        refs = refs[len(FRONT[part]):]
    for part in range(parts):
        siblings.append(refs[:len(BACK[part])])
        refs = refs[len(siblings[part]):] if part < parts - 1 else refs
    mixed_ref, squares_ref = refs[-2:]
    core, chip, _, _ = place()
    rows, width = query_ref.shape
    use = use_ref[...]
    squares = jnp.zeros((rows, HD), F32)
    order = steps(width)
    first = len(order) - len(part_steps(width, parts - 1, BACK[-1][-1]))
    for i, step in enumerate(order):
        found = [intras[which][:, tile(at)] for which, at in sources[i]]
        both = found[0] if sources[i][0] == sources[i][1] else jnp.where(core == 0, *found)
        own, part, k, j = step
        size = sizes(width)[part]
        spot = QUARTERS.index(k)
        if own:
            which, at = found_in(FRONT[part], spot)
            state = weight("mix_scale") * states[part][spot][tile(j), :]
            state = state + weight("mix_add") * gots[part][which][tile(at * size + j), :]
            past = from_past(use, query_ref, step, state)
        elif i < first:
            which, at = found_in(BACK[part], spot)
            past = use * siblings[part][which][:, tile(at * size + j)]
        else:
            mixed_ref[:, tile(i)] = both
            continue
        both = both + past
        squares = squares + both * both
        mixed_ref[:, tile(i)] = both * gain_ref[:, column(width, core, chip, *step)]
    squares_ref[...] = squares


def norm_kernel(use_ref, gain_ref, mixed_ref, squares_ref, sibling_ref, out_hbm, out_ref, sems):
    core, chip, _, _ = place()
    rows, width = out_ref.shape
    order = steps(width)
    first = len(order) - sibling_ref.shape[1] // HD
    use = use_ref[...]
    squares = squares_ref[...]
    late = []
    for i, step in enumerate(order[first:]):
        both = mixed_ref[:, tile(first + i)] + use * sibling_ref[:, tile(i)]
        squares = squares + both * both
        late.append(both * gain_ref[:, column(width, core, chip, *step)])
    mean = jnp.sum(squares, axis=-1, keepdims=True) * (1.0 / width)
    norm = jnp.broadcast_to(lax.rsqrt(mean + 1e-05), (rows, HD))
    copies = []
    number = sems.shape[0]
    for part in range(number):
        at = slice(part * rows // number, (part + 1) * rows // number)
        for i, step in enumerate(order):
            both = mixed_ref[at, tile(i)] if i < first else late[i - first][at, :]
            out_ref[at, column(width, core, chip, *step)] = (both * norm[at, :]).astype(BF16)
        copies.append(pltpu.make_async_copy(out_ref.at[at, :], out_hbm.at[at, :], sems.at[part]))
        copies[-1].start()
    for copy in copies:
        copy.wait()


def in_hbm(array):
    return pltpu.with_memory_space_constraint(array, pltpu.HBM)


def array(shape, dtype=F32):
    return jax.ShapeDtypeStruct(shape, dtype)


def shards(count, query_rows, key_rows, value_rows, seg_starts, norm_gain):
    query, key, value = query_rows[0], key_rows[0], value_rows[0]
    rows, width = query.shape
    groups = count // (2 * CHIPS)
    parts = range(len(SPLIT))
    heads = len(steps(width))
    lanes = [array((size * HD, HD)) for size in sizes(width)]

    def tall(part, spots):
        return array((len(part_steps(width, part, spots)) * HD, HD))

    def call(kernel, outs, *args, scratch=()):
        return pl.pallas_call(
            kernel, out_shape=outs, in_specs=[VM] * len(args), out_specs=jax.tree.map(lambda _: VM, outs),
            scratch_shapes=scratch, compiler_params=PARAMS,
        )(*args)

    def weighted(kernel, outs, *args):
        def body(table_ref, *refs):
            return kernel(functools.partial(row, table_ref, groups), *refs)

        return call(body, outs, table, *args)

    def swap(what, bits):
        return lax.ppermute(what, "ctx", [(i, i ^ bits) for i in range(count)])

    def later(what, shift):
        return lax.ppermute(what, "ctx", [(i, (i + shift * 2 * CHIPS) % count) for i in range(count)])

    def intra(on, span, *after):
        out = array((rows, (span[1] - span[0]) * HD))
        return call(functools.partial(intra_kernel, on, span), out, allowed, query, key, value, *after)

    def summary(what, *after):
        outs = [tall(*step[1:]) for step in what]
        return call(functools.partial(summary_kernel, what), outs, kept, key, value, *after)

    key, value, table, kept, allowed, use, *sends = pl.pallas_call(
        functools.partial(first_kernel, groups),
        out_shape=[array((rows, width), BF16)] * 2 + [
            array((-(-len(table_rows(groups)) // 8) * 8, HD)), array((rows, HD), BF16), array((rows, rows)),
            array((rows, HD))] + [tall(0, spots) for spots in FRONT[0]],
        in_specs=[HB] * 3, out_specs=[VM] * (6 + len(FRONT[0])),
        scratch_shapes=[pltpu.SMEM(seg_starts.shape, jnp.int32), pltpu.SemaphoreType.DMA((3,))],
        compiler_params=PARAMS,
    )(in_hbm(seg_starts), in_hbm(key), in_hbm(value))
    gots, keeps = [], []
    for part in parts:
        gots.append([swap(send, 1) for send in sends])
        keep = [(True, part, spots) for spots in FRONT[part]]
        send = [(False, part + 1, spots) for spots in FRONT[part + 1]] if part + 1 < len(SPLIT) else []
        outs = summary(keep + send)
        keeps.append(outs[:len(keep)])
        sends = outs[len(keep):]
    done = [[None] * heads, [None] * heads]
    intras = []

    def inside(slot, *after):
        new = []
        for on, span in SLOTS.get(slot, ()):
            span = tuple(heads * at // 32 for at in span)
            for core in range(2) if on is None else (on,):
                done[core][slice(*span)] = [(len(intras), i) for i in range(span[1] - span[0])]
            intras.append(intra(on, span, *after))
            new.append(intras[-1])
        return new

    chips, totals, states, siblings = [{} for _ in range(4)]

    def begin(part, *after):
        own = {}
        for spots, keep, got in zip(FRONT[part], keeps[part], gots[part]):
            outs = weighted(
                functools.partial(chip_kernel, len(spots)), [lanes[part]] * len(spots), keep, got, *after)
            own.update(zip(spots, outs))
        chips[part] = {spot: swap(own[spot], 2 * QUARTERS[spot]) if QUARTERS[spot] else own[spot] for spot in own}
        return chips[part]

    def between(part, *after):
        total = weighted(total_kernel, lanes[part], *[chips[part][spot] for spot in range(CHIPS)], *after)
        totals[part] = [later(total, shift) for shift in range(1, groups)]
        return [total]

    def enter(part, *after):
        outs = weighted(
            functools.partial(straight_kernel, groups - 1), [lanes[part]] * CHIPS,
            *[chips[part][spot] for spot in range(CHIPS)], *totals[part], *after)
        states[part] = [swap(out, 2 * k) if k else out for out, k in zip(outs, QUARTERS)]
        return [outs[0]]

    def share(part, *after):
        siblings[part] = []
        for spots in BACK[part]:
            siblings[part].append(swap(weighted(
                functools.partial(pair_kernel, part, spots), array((rows, tall(part, spots).shape[0])), *keeps[part],
                *[states[part][spot] for spot in spots], asked, *after), 1))
        return siblings[part][:1]

    asked = swap(call(query_kernel, array((rows, width // 2)), query), 1)
    a = begin(0, *inside("start", keeps[0][0]))
    b = begin(1, a[1], asked)
    a = between(0, *inside("begin", b[0]))
    b = between(1, *inside("between", a[0]))
    a = enter(0, *inside("between1", b[0]))
    b = enter(1, *inside("enter", a[0]))
    a = share(0, *inside("enter1", b[0]))
    b = share(1, *inside("share", a[0]))
    siblings, states = [siblings[part] for part in parts], [states[part] for part in parts]
    gain = norm_gain[None, :]
    mixed, squares = weighted(
        functools.partial(mix_kernel, list(zip(*done)), len(intras)), [array((rows, width)), array((rows, HD))], use, query, gain,
        *intras, *[piece for state in states for piece in state], *[got for group in gots for got in group],
        *[sibling for group in siblings for sibling in group][:-1])
    attended = pl.pallas_call(
        norm_kernel, out_shape=array((rows, width), BF16), in_specs=[VM] * 5, out_specs=HB,
        scratch_shapes=[pltpu.VMEM((rows, width), BF16), pltpu.SemaphoreType.DMA((4,))], compiler_params=PARAMS,
    )(use, gain, mixed, squares, siblings[-1][-1])
    return attended[None]


def solution(mesh):
    placed = (
        P("sess", "ctx", None),
        P("sess", "ctx", None),
        P("sess", "ctx", None),
        P("sess", None),
        P(),
    )
    return jax.shard_map(
        functools.partial(shards, mesh.shape["ctx"]), mesh=mesh, in_specs=placed,
        out_specs=P("sess", "ctx", None), check_vma=False
    )
```

```python
import functools

import jax
import jax.numpy as jnp
from jax import lax
from jax.experimental import pallas as pl
from jax.experimental.pallas import tpu as pltpu
from jax.sharding import PartitionSpec as P

HD = 128
CHIPS = 4
QUARTERS = (0, 3, 2, 1)
FRONT = (((0, 1, 2, 3),), ((0, 1, 2, 3),))
BACK = (((0, 1, 2, 3),), ((0, 1, 2, 3),))
SPLIT = (1, 1)
SLOTS = {'start': [(0, (0, 12))], 'enter1': [(0, (12, 32)), (1, (0, 32))]}
F32 = jnp.float32
BF16 = jnp.bfloat16
HB = pl.BlockSpec(memory_space=pltpu.HBM)
SM = pl.BlockSpec(memory_space=pltpu.SMEM)
VM = pl.BlockSpec(memory_space=pltpu.VMEM)
PARAMS = pltpu.CompilerParams(vmem_limit_bytes=32 * 1024 * 1024)


def place():
    block = lax.axis_index("ctx")
    return block % 2, (block // 2) % CHIPS, block // (2 * CHIPS), block


def segment_at(starts, position):
    count = jnp.int32(0)
    for i in range(starts.shape[1]):
        count = count + (starts[0, i] <= position).astype(jnp.int32)
    return count


def same(starts, rows, late, early):
    one = segment_at(starts, (late + 1) * rows - 1)
    two = segment_at(starts, (early + 1) * rows - 1)
    return (one == two).astype(F32)


def segment_rows(starts, positions):
    count = jnp.zeros(positions.shape, jnp.int32)
    for i in range(starts.shape[1]):
        count = count + (starts[0, i] <= positions).astype(jnp.int32)
    return count


def tile(index):
    return slice(index * HD, (index + 1) * HD)


def sizes(width):
    quarter = width // HD // 2 // CHIPS
    return [quarter * share // sum(SPLIT) for share in SPLIT]


def part_steps(width, part, spots=range(CHIPS)):
    return [(part, QUARTERS[spot], j) for spot in spots for j in range(sizes(width)[part])]


def steps(width):
    return [
        (own, *step) for own in (True, False) for part in range(len(SPLIT)) for spots in BACK[part]
        for step in part_steps(width, part, spots)]


def found_in(groups, spot):
    return next((i, group.index(spot)) for i, group in enumerate(groups) if spot in group)


def column(width, core, chip, own, part, k, j):
    parts = sizes(width)
    quarter = sum(parts)
    half = core if own else 1 - core
    head = (half * CHIPS + lax.bitwise_xor(chip, k)) * quarter + sum(parts[:part]) + j
    return pl.ds(pl.multiple_of(head * HD, HD), HD)


def table_rows(groups):
    names = ["chip_mine", "chip_other", "pair_scale", "pair_add", "mix_scale", "mix_add"]
    names += [("total", k) for k in range(CHIPS)]
    names += [("carry", k, j) for k in range(CHIPS) for j in range(CHIPS)]
    names += [("enter", k) for k in range(CHIPS)]
    names += [("before", s) for s in range(groups - 1)]
    return {name: i for i, name in enumerate(names)}


def weights(starts, rows, groups):
    core, chip, group, block = place()
    same_ = functools.partial(same, starts, rows)
    mine, first = block // 2 * 2, group * 2 * CHIPS
    joined = same_(mine + 1, mine)
    after, mix = same_(block, block - 1), same_(block - 1, block - 2)
    found = {
        "chip_mine": jnp.where(core == 0, joined, 1.0),
        "chip_other": jnp.where(core == 0, 1.0, joined),
        "pair_scale": jnp.where(core == 0, after, 1.0),
        "pair_add": jnp.where(core == 0, 1.0, 0.0),
        "mix_scale": jnp.where(core == 0, 1.0, mix),
        "mix_add": jnp.where(core == 0, 0.0, 1.0),
    }
    for k in range(CHIPS):
        target = lax.bitwise_xor(chip, k)
        end = first + 2 * target - 1
        found["total", k] = same_(first + 7, first + 2 * target + 1)
        found["enter", k] = same_(end, first - 1)
        for j in range(CHIPS):
            source = lax.bitwise_xor(chip, j)
            found["carry", k, j] = jnp.where(source < target, same_(end, first + 2 * source + 1), 0.0)
    for s in range(groups - 1):
        end = first - 1 - s * 2 * CHIPS
        found["before", s] = jnp.where(end >= 0, same_(first - 1, end), 0.0)
    return found


def summarize(kept_ref, key_ref, value_ref, own, part, spots, out):
    core, chip, _, _ = place()
    width = key_ref.shape[1]
    kept = kept_ref[...]
    for i, step in enumerate(part_steps(width, part, spots)):
        at = column(width, core, chip, own, *step)
        out[tile(i), :] = lax.dot_general(
            key_ref[:, at] * kept, value_ref[:, at], (((0,), (0,)), ((), ())), preferred_element_type=F32)


def first_kernel(groups, starts_hbm, key_hbm, value_hbm, table_ref, kept_ref, allowed_ref, use_ref, send_ref, starts,
                 key_ref, value_ref, sems):
    core, chip, _, block = place()
    rows, width = key_hbm.shape
    copies = [pltpu.make_async_copy(starts_hbm, starts, sems.at[0])]
    todo = part_steps(width, 0)
    size = sizes(width)[0]
    for i, step in enumerate(todo[::size]):
        at = pl.ds(column(width, core, chip, False, *step).start, size * HD)
        to = slice(i * size * HD, (i + 1) * size * HD)
        for source, target in ((key_hbm, key_ref), (value_hbm, value_ref)):
            copies.append(pltpu.make_async_copy(source.at[:, at], target.at[:, to], sems.at[len(copies)]))
    for copy in copies:
        copy.start()
    copies[0].wait()
    begin = block * rows
    names = table_rows(groups)
    for name, weight in weights(starts, rows, groups).items():
        table_ref[names[name]:names[name] + 1, :] = jnp.full((1, HD), weight, F32)
    segments = segment_rows(starts, begin + lax.broadcasted_iota(jnp.int32, (rows, HD), 0))
    kept = (segments == segment_at(starts, begin + rows - 1)).astype(F32).astype(BF16)
    kept_ref[...] = kept
    use_ref[...] = (segments == segment_at(starts, begin - 1)).astype(F32)
    late = begin + lax.broadcasted_iota(jnp.int32, (rows, rows), 0)
    early = begin + lax.broadcasted_iota(jnp.int32, (rows, rows), 1)
    allowed = (late >= early) & (segment_rows(starts, late) == segment_rows(starts, early))
    allowed_ref[...] = allowed.astype(F32)
    for copy in copies[1:]:
        copy.wait()
    for i in range(len(todo)):
        send_ref[tile(i), :] = lax.dot_general(
            key_ref[:, tile(i)] * kept, value_ref[:, tile(i)], (((0,), (0,)), ((), ())), preferred_element_type=F32)


def summary_kernel(what, kept_ref, key_ref, value_ref, *refs):
    for (own, part, spots), out in zip(what, refs[-len(what):]):
        summarize(kept_ref, key_ref, value_ref, own, part, spots, out)


def row(table_ref, groups, *name):
    at = table_rows(groups)[name if len(name) > 1 else name[0]]
    return table_ref[at:at + 1, :]


def chip_kernel(count, weight, keep_ref, got_ref, *refs):
    size = refs[-1].shape[0]
    for i, out in enumerate(refs[-count:]):
        at = slice(i * size, (i + 1) * size)
        out[...] = weight("chip_mine") * keep_ref[at, :] + weight("chip_other") * got_ref[at, :]


def total_kernel(weight, *refs):
    total = None
    for k, piece in zip(QUARTERS, refs[:CHIPS]):
        term = weight("total", k) * piece[...]
        total = term if total is None else total + term
    refs[-1][...] = total


def straight_kernel(shifts, weight, *refs):
    pieces, outs = refs[:CHIPS], refs[-CHIPS:]
    before = entered(weight, refs[CHIPS:CHIPS + shifts])
    for k, out in zip(QUARTERS, outs):
        state = weight("enter", k) * before
        for j, piece in zip(QUARTERS, pieces):
            if j != k:
                state = state + weight("carry", k, j) * piece[...]
        out[...] = state


def entered(weight, totals):
    before = None
    for s, total in enumerate(totals):
        term = weight("before", s) * total[...]
        before = term if before is None else before + term
    return before


def query_kernel(query_ref, *refs):
    core, chip, _, _ = place()
    width = query_ref.shape[1]
    order = steps(width)
    half = len(order) // 2
    for i, step in enumerate(order[half:]):
        refs[-1][:, tile(i)] = query_ref[:, column(width, core, chip, *step)].astype(F32)


def pair_kernel(part, spots, weight, *refs):
    keeps, pieces = refs[:len(FRONT[part])], refs[len(FRONT[part]):][:len(spots)]
    query_ref, out = refs[len(keeps) + len(spots)], refs[-1]
    width = 2 * query_ref.shape[1]
    order = steps(width)
    size = pieces[0].shape[0]
    for i, (spot, piece) in enumerate(zip(spots, pieces)):
        which, place_in = found_in(FRONT[part], spot)
        keep = keeps[which][place_in * size:(place_in + 1) * size, :]
        state = (weight("pair_scale") * piece[...] + weight("pair_add") * keep).astype(BF16)
        for j in range(size // HD):
            query = query_ref[:, tile(order.index((True, part, QUARTERS[spot], j)))].astype(BF16)
            out[:, tile(i * (size // HD) + j)] = jnp.dot(query, state[tile(j), :], preferred_element_type=F32)


def intra_kernel(on, span, allowed_ref, query_ref, key_ref, value_ref, *refs):
    out_ref = refs[-1]
    core, chip, _, _ = place()
    width = query_ref.shape[1]

    def body():
        allowed = allowed_ref[...]
        for i, step in enumerate(steps(width)[slice(*span)]):
            at = column(width, core, chip, *step)
            scores = lax.dot_general(
                query_ref[:, at], key_ref[:, at], (((1,), (1,)), ((), ())), preferred_element_type=F32)
            out_ref[:, tile(i)] = jnp.dot(
                (scores * allowed).astype(BF16), value_ref[:, at], preferred_element_type=F32)

    if on is None:
        body()
    else:
        pl.when(core == on)(body)


def from_past(use, query_ref, step, state):
    core, chip, _, _ = place()
    at = column(query_ref.shape[1], core, chip, *step)
    return use * jnp.dot(query_ref[:, at], state.astype(BF16), preferred_element_type=F32)


def mix_kernel(sources, count, weight, use_ref, query_ref, gain_ref, *refs):
    parts = len(SPLIT)
    intras, refs = refs[:count], refs[count:]
    states = [refs[part * CHIPS:(part + 1) * CHIPS] for part in range(parts)]
    refs = refs[parts * CHIPS:]
    gots, siblings = [], []
    for part in range(parts):
        gots.append(refs[:len(FRONT[part])])
        refs = refs[len(FRONT[part]):]
    for part in range(parts):
        siblings.append(refs[:len(BACK[part])])
        refs = refs[len(siblings[part]):] if part < parts - 1 else refs
    mixed_ref, squares_ref = refs[-2:]
    core, chip, _, _ = place()
    rows, width = query_ref.shape
    use = use_ref[...]
    squares = jnp.zeros((rows, HD), F32)
    order = steps(width)
    first = len(order) - len(part_steps(width, parts - 1, BACK[-1][-1]))
    for i, step in enumerate(order):
        found = [intras[which][:, tile(at)] for which, at in sources[i]]
        both = found[0] if sources[i][0] == sources[i][1] else jnp.where(core == 0, *found)
        own, part, k, j = step
        size = sizes(width)[part]
        spot = QUARTERS.index(k)
        if own:
            which, at = found_in(FRONT[part], spot)
            state = weight("mix_scale") * states[part][spot][tile(j), :]
            state = state + weight("mix_add") * gots[part][which][tile(at * size + j), :]
            past = from_past(use, query_ref, step, state)
        elif i < first:
            which, at = found_in(BACK[part], spot)
            past = use * siblings[part][which][:, tile(at * size + j)]
        else:
            mixed_ref[:, tile(i)] = both
            continue
        both = both + past
        squares = squares + both * both
        mixed_ref[:, tile(i)] = both * gain_ref[:, column(width, core, chip, *step)]
    squares_ref[...] = squares


def norm_kernel(use_ref, gain_ref, mixed_ref, squares_ref, sibling_ref, out_hbm, out_ref, sems):
    core, chip, _, _ = place()
    rows, width = out_ref.shape
    order = steps(width)
    first = len(order) - sibling_ref.shape[1] // HD
    use = use_ref[...]
    squares = squares_ref[...]
    late = []
    for i, step in enumerate(order[first:]):
        both = mixed_ref[:, tile(first + i)] + use * sibling_ref[:, tile(i)]
        squares = squares + both * both
        late.append(both * gain_ref[:, column(width, core, chip, *step)])
    mean = jnp.sum(squares, axis=-1, keepdims=True) * (1.0 / width)
    norm = jnp.broadcast_to(lax.rsqrt(mean + 1e-05), (rows, HD))
    copies = []
    number = sems.shape[0]
    for part in range(number):
        at = slice(part * rows // number, (part + 1) * rows // number)
        for i, step in enumerate(order):
            both = mixed_ref[at, tile(i)] if i < first else late[i - first][at, :]
            out_ref[at, column(width, core, chip, *step)] = (both * norm[at, :]).astype(BF16)
        copies.append(pltpu.make_async_copy(out_ref.at[at, :], out_hbm.at[at, :], sems.at[part]))
        copies[-1].start()
    for copy in copies:
        copy.wait()


def in_hbm(array):
    return pltpu.with_memory_space_constraint(array, pltpu.HBM)


def array(shape, dtype=F32):
    return jax.ShapeDtypeStruct(shape, dtype)


def shards(count, query_rows, key_rows, value_rows, seg_starts, norm_gain):
    query, key, value = query_rows[0], key_rows[0], value_rows[0]
    rows, width = query.shape
    groups = count // (2 * CHIPS)
    parts = range(len(SPLIT))
    heads = len(steps(width))
    lanes = [array((size * HD, HD)) for size in sizes(width)]

    def tall(part, spots):
        return array((len(part_steps(width, part, spots)) * HD, HD))

    def call(kernel, outs, *args, scratch=()):
        return pl.pallas_call(
            kernel, out_shape=outs, in_specs=[VM] * len(args), out_specs=jax.tree.map(lambda _: VM, outs),
            scratch_shapes=scratch, compiler_params=PARAMS,
        )(*args)

    def weighted(kernel, outs, *args):
        def body(table_ref, *refs):
            return kernel(functools.partial(row, table_ref, groups), *refs)

        return call(body, outs, table, *args)

    def swap(what, bits):
        return lax.ppermute(what, "ctx", [(i, i ^ bits) for i in range(count)])

    def later(what, shift):
        return lax.ppermute(what, "ctx", [(i, (i + shift * 2 * CHIPS) % count) for i in range(count)])

    def intra(on, span, *after):
        out = array((rows, (span[1] - span[0]) * HD))
        return call(functools.partial(intra_kernel, on, span), out, allowed, query, key, value, *after)

    def summary(what, *after):
        outs = [tall(*step[1:]) for step in what]
        return call(functools.partial(summary_kernel, what), outs, kept, key, value, *after)

    some = pltpu.VMEM((rows, sizes(width)[0] * CHIPS * HD), BF16)
    table, kept, allowed, use, *sends = pl.pallas_call(
        functools.partial(first_kernel, groups),
        out_shape=[
            array((-(-len(table_rows(groups)) // 8) * 8, HD)), array((rows, HD), BF16), array((rows, rows)),
            array((rows, HD)), tall(0, range(CHIPS))],
        in_specs=[HB] * 3, out_specs=[VM] * 5,
        scratch_shapes=[
            pltpu.SMEM(seg_starts.shape, jnp.int32), some, some, pltpu.SemaphoreType.DMA((1 + 2 * CHIPS,))],
        compiler_params=PARAMS,
    )(in_hbm(seg_starts), in_hbm(key), in_hbm(value))
    gots, keeps = [], []
    for part in parts:
        gots.append([swap(send, 1) for send in sends])
        keep = [(True, part, spots) for spots in FRONT[part]]
        send = [(False, part + 1, spots) for spots in FRONT[part + 1]] if part + 1 < len(SPLIT) else []
        outs = summary(keep + send)
        keeps.append(outs[:len(keep)])
        sends = outs[len(keep):]
    done = [[None] * heads, [None] * heads]
    intras = []

    def inside(slot, *after):
        new = []
        for on, span in SLOTS.get(slot, ()):
            span = tuple(heads * at // 32 for at in span)
            for core in range(2) if on is None else (on,):
                done[core][slice(*span)] = [(len(intras), i) for i in range(span[1] - span[0])]
            intras.append(intra(on, span, *after))
            new.append(intras[-1])
        return new

    chips, totals, states, siblings = [{} for _ in range(4)]

    def begin(part, *after):
        own = {}
        for spots, keep, got in zip(FRONT[part], keeps[part], gots[part]):
            outs = weighted(
                functools.partial(chip_kernel, len(spots)), [lanes[part]] * len(spots), keep, got, *after)
            own.update(zip(spots, outs))
        chips[part] = {spot: swap(own[spot], 2 * QUARTERS[spot]) if QUARTERS[spot] else own[spot] for spot in own}
        return chips[part]

    def between(part, *after):
        total = weighted(total_kernel, lanes[part], *[chips[part][spot] for spot in range(CHIPS)], *after)
        totals[part] = [later(total, shift) for shift in range(1, groups)]
        return [total]

    def enter(part, *after):
        outs = weighted(
            functools.partial(straight_kernel, groups - 1), [lanes[part]] * CHIPS,
            *[chips[part][spot] for spot in range(CHIPS)], *totals[part], *after)
        states[part] = [swap(out, 2 * k) if k else out for out, k in zip(outs, QUARTERS)]
        return [outs[0]]

    def share(part, *after):
        siblings[part] = []
        for spots in BACK[part]:
            siblings[part].append(swap(weighted(
                functools.partial(pair_kernel, part, spots), array((rows, tall(part, spots).shape[0])), *keeps[part],
                *[states[part][spot] for spot in spots], asked, *after), 1))
        return siblings[part][:1]

    asked = swap(call(query_kernel, array((rows, width // 2)), query), 1)
    a = begin(0, *inside("start", keeps[0][0]))
    b = begin(1, a[1], asked)
    a = between(0, *inside("begin", b[0]))
    b = between(1, *inside("between", a[0]))
    a = enter(0, *inside("between1", b[0]))
    b = enter(1, *inside("enter", a[0]))
    a = share(0, *inside("enter1", b[0]))
    b = share(1, *inside("share", a[0]))
    siblings, states = [siblings[part] for part in parts], [states[part] for part in parts]
    gain = norm_gain[None, :]
    mixed, squares = weighted(
        functools.partial(mix_kernel, list(zip(*done)), len(intras)), [array((rows, width)), array((rows, HD))], use, query, gain,
        *intras, *[piece for state in states for piece in state], *[got for group in gots for got in group],
        *[sibling for group in siblings for sibling in group][:-1])
    attended = pl.pallas_call(
        norm_kernel, out_shape=array((rows, width), BF16), in_specs=[VM] * 5, out_specs=HB,
        scratch_shapes=[pltpu.VMEM((rows, width), BF16), pltpu.SemaphoreType.DMA((4,))], compiler_params=PARAMS,
    )(use, gain, mixed, squares, siblings[-1][-1])
    return attended[None]


def solution(mesh):
    placed = (
        P("sess", "ctx", None),
        P("sess", "ctx", None),
        P("sess", "ctx", None),
        P("sess", None),
        P(),
    )
    return jax.shard_map(
        functools.partial(shards, mesh.shape["ctx"]), mesh=mesh, in_specs=placed,
        out_specs=P("sess", "ctx", None), check_vma=False
    )
```

```python
import functools

import jax
import jax.numpy as jnp
from jax import lax
from jax.experimental import pallas as pl
from jax.experimental.pallas import tpu as pltpu
from jax.sharding import PartitionSpec as P

HD = 128
CHIPS = 4
QUARTERS = (0, 3, 2, 1)
FRONT = (((0, 1, 2, 3),), ((0, 1, 2, 3),))
BACK = (((0, 1, 2, 3),), ((0, 1, 2, 3),))
SPLIT = (1, 1)
SLOTS = {'start': [(0, (0, 12))], 'between': [(0, (12, 24))], 'enter1': [(0, (24, 32)), (1, (0, 32))]}
F32 = jnp.float32
BF16 = jnp.bfloat16
HB = pl.BlockSpec(memory_space=pltpu.HBM)
SM = pl.BlockSpec(memory_space=pltpu.SMEM)
VM = pl.BlockSpec(memory_space=pltpu.VMEM)
PARAMS = pltpu.CompilerParams(vmem_limit_bytes=32 * 1024 * 1024)


def place():
    block = lax.axis_index("ctx")
    return block % 2, (block // 2) % CHIPS, block // (2 * CHIPS), block


def segment_at(starts, position):
    count = jnp.int32(0)
    for i in range(starts.shape[1]):
        count = count + (starts[0, i] <= position).astype(jnp.int32)
    return count


def same(starts, rows, late, early):
    one = segment_at(starts, (late + 1) * rows - 1)
    two = segment_at(starts, (early + 1) * rows - 1)
    return (one == two).astype(F32)


def segment_rows(starts, positions):
    count = jnp.zeros(positions.shape, jnp.int32)
    for i in range(starts.shape[1]):
        count = count + (starts[0, i] <= positions).astype(jnp.int32)
    return count


def tile(index):
    return slice(index * HD, (index + 1) * HD)


def sizes(width):
    quarter = width // HD // 2 // CHIPS
    return [quarter * share // sum(SPLIT) for share in SPLIT]


def part_steps(width, part, spots=range(CHIPS)):
    return [(part, QUARTERS[spot], j) for spot in spots for j in range(sizes(width)[part])]


def steps(width):
    return [
        (own, *step) for own in (True, False) for part in range(len(SPLIT)) for spots in BACK[part]
        for step in part_steps(width, part, spots)]


def found_in(groups, spot):
    return next((i, group.index(spot)) for i, group in enumerate(groups) if spot in group)


def column(width, core, chip, own, part, k, j):
    parts = sizes(width)
    quarter = sum(parts)
    half = core if own else 1 - core
    head = (half * CHIPS + lax.bitwise_xor(chip, k)) * quarter + sum(parts[:part]) + j
    return pl.ds(pl.multiple_of(head * HD, HD), HD)


def table_rows(groups):
    names = ["chip_mine", "chip_other", "pair_scale", "pair_add", "mix_scale", "mix_add"]
    names += [("total", k) for k in range(CHIPS)]
    names += [("carry", k, j) for k in range(CHIPS) for j in range(CHIPS)]
    names += [("enter", k) for k in range(CHIPS)]
    names += [("before", s) for s in range(groups - 1)]
    return {name: i for i, name in enumerate(names)}


def weights(starts, rows, groups):
    core, chip, group, block = place()
    same_ = functools.partial(same, starts, rows)
    mine, first = block // 2 * 2, group * 2 * CHIPS
    joined = same_(mine + 1, mine)
    after, mix = same_(block, block - 1), same_(block - 1, block - 2)
    found = {
        "chip_mine": jnp.where(core == 0, joined, 1.0),
        "chip_other": jnp.where(core == 0, 1.0, joined),
        "pair_scale": jnp.where(core == 0, after, 1.0),
        "pair_add": jnp.where(core == 0, 1.0, 0.0),
        "mix_scale": jnp.where(core == 0, 1.0, mix),
        "mix_add": jnp.where(core == 0, 0.0, 1.0),
    }
    for k in range(CHIPS):
        target = lax.bitwise_xor(chip, k)
        end = first + 2 * target - 1
        found["total", k] = same_(first + 7, first + 2 * target + 1)
        found["enter", k] = same_(end, first - 1)
        for j in range(CHIPS):
            source = lax.bitwise_xor(chip, j)
            found["carry", k, j] = jnp.where(source < target, same_(end, first + 2 * source + 1), 0.0)
    for s in range(groups - 1):
        end = first - 1 - s * 2 * CHIPS
        found["before", s] = jnp.where(end >= 0, same_(first - 1, end), 0.0)
    return found


def summarize(kept_ref, key_ref, value_ref, own, part, spots, out):
    core, chip, _, _ = place()
    width = key_ref.shape[1]
    kept = kept_ref[...]
    for i, step in enumerate(part_steps(width, part, spots)):
        at = column(width, core, chip, own, *step)
        out[tile(i), :] = lax.dot_general(
            key_ref[:, at] * kept, value_ref[:, at], (((0,), (0,)), ((), ())), preferred_element_type=F32)


def first_kernel(groups, starts_hbm, key_hbm, value_hbm, table_ref, kept_ref, allowed_ref, use_ref, send_ref, starts,
                 key_ref, value_ref, sems):
    core, chip, _, block = place()
    rows, width = key_hbm.shape
    copies = [pltpu.make_async_copy(starts_hbm, starts, sems.at[0])]
    todo = part_steps(width, 0)
    size = sizes(width)[0]
    for i, step in enumerate(todo[::size]):
        at = pl.ds(column(width, core, chip, False, *step).start, size * HD)
        to = slice(i * size * HD, (i + 1) * size * HD)
        for source, target in ((key_hbm, key_ref), (value_hbm, value_ref)):
            copies.append(pltpu.make_async_copy(source.at[:, at], target.at[:, to], sems.at[len(copies)]))
    for copy in copies:
        copy.start()
    copies[0].wait()
    begin = block * rows
    names = table_rows(groups)
    for name, weight in weights(starts, rows, groups).items():
        table_ref[names[name]:names[name] + 1, :] = jnp.full((1, HD), weight, F32)
    segments = segment_rows(starts, begin + lax.broadcasted_iota(jnp.int32, (rows, HD), 0))
    kept = (segments == segment_at(starts, begin + rows - 1)).astype(F32).astype(BF16)
    kept_ref[...] = kept
    use_ref[...] = (segments == segment_at(starts, begin - 1)).astype(F32)
    late = begin + lax.broadcasted_iota(jnp.int32, (rows, rows), 0)
    early = begin + lax.broadcasted_iota(jnp.int32, (rows, rows), 1)
    allowed = (late >= early) & (segment_rows(starts, late) == segment_rows(starts, early))
    allowed_ref[...] = allowed.astype(F32)
    for copy in copies[1:]:
        copy.wait()
    for i in range(len(todo)):
        send_ref[tile(i), :] = lax.dot_general(
            key_ref[:, tile(i)] * kept, value_ref[:, tile(i)], (((0,), (0,)), ((), ())), preferred_element_type=F32)


def summary_kernel(what, kept_ref, key_ref, value_ref, *refs):
    for (own, part, spots), out in zip(what, refs[-len(what):]):
        summarize(kept_ref, key_ref, value_ref, own, part, spots, out)


def row(table_ref, groups, *name):
    at = table_rows(groups)[name if len(name) > 1 else name[0]]
    return table_ref[at:at + 1, :]


def chip_kernel(count, weight, keep_ref, got_ref, *refs):
    size = refs[-1].shape[0]
    for i, out in enumerate(refs[-count:]):
        at = slice(i * size, (i + 1) * size)
        out[...] = weight("chip_mine") * keep_ref[at, :] + weight("chip_other") * got_ref[at, :]


def total_kernel(weight, *refs):
    total = None
    for k, piece in zip(QUARTERS, refs[:CHIPS]):
        term = weight("total", k) * piece[...]
        total = term if total is None else total + term
    refs[-1][...] = total


def straight_kernel(shifts, weight, *refs):
    pieces, outs = refs[:CHIPS], refs[-CHIPS:]
    before = entered(weight, refs[CHIPS:CHIPS + shifts])
    for k, out in zip(QUARTERS, outs):
        state = weight("enter", k) * before
        for j, piece in zip(QUARTERS, pieces):
            if j != k:
                state = state + weight("carry", k, j) * piece[...]
        out[...] = state


def entered(weight, totals):
    before = None
    for s, total in enumerate(totals):
        term = weight("before", s) * total[...]
        before = term if before is None else before + term
    return before


def query_kernel(query_ref, *refs):
    core, chip, _, _ = place()
    width = query_ref.shape[1]
    order = steps(width)
    half = len(order) // 2
    for i, step in enumerate(order[half:]):
        refs[-1][:, tile(i)] = query_ref[:, column(width, core, chip, *step)].astype(F32)


def pair_kernel(part, spots, weight, *refs):
    keeps, pieces = refs[:len(FRONT[part])], refs[len(FRONT[part]):][:len(spots)]
    query_ref, out = refs[len(keeps) + len(spots)], refs[-1]
    width = 2 * query_ref.shape[1]
    order = steps(width)
    size = pieces[0].shape[0]
    for i, (spot, piece) in enumerate(zip(spots, pieces)):
        which, place_in = found_in(FRONT[part], spot)
        keep = keeps[which][place_in * size:(place_in + 1) * size, :]
        state = (weight("pair_scale") * piece[...] + weight("pair_add") * keep).astype(BF16)
        for j in range(size // HD):
            query = query_ref[:, tile(order.index((True, part, QUARTERS[spot], j)))].astype(BF16)
            out[:, tile(i * (size // HD) + j)] = jnp.dot(query, state[tile(j), :], preferred_element_type=F32)


def intra_kernel(on, span, allowed_ref, query_ref, key_ref, value_ref, *refs):
    out_ref = refs[-1]
    core, chip, _, _ = place()
    width = query_ref.shape[1]

    def body():
        allowed = allowed_ref[...]
        for i, step in enumerate(steps(width)[slice(*span)]):
            at = column(width, core, chip, *step)
            scores = lax.dot_general(
                query_ref[:, at], key_ref[:, at], (((1,), (1,)), ((), ())), preferred_element_type=F32)
            out_ref[:, tile(i)] = jnp.dot(
                (scores * allowed).astype(BF16), value_ref[:, at], preferred_element_type=F32)

    if on is None:
        body()
    else:
        pl.when(core == on)(body)


def from_past(use, query_ref, step, state):
    core, chip, _, _ = place()
    at = column(query_ref.shape[1], core, chip, *step)
    return use * jnp.dot(query_ref[:, at], state.astype(BF16), preferred_element_type=F32)


def mix_kernel(sources, count, weight, use_ref, query_ref, gain_ref, *refs):
    parts = len(SPLIT)
    intras, refs = refs[:count], refs[count:]
    states = [refs[part * CHIPS:(part + 1) * CHIPS] for part in range(parts)]
    refs = refs[parts * CHIPS:]
    gots, siblings = [], []
    for part in range(parts):
        gots.append(refs[:len(FRONT[part])])
        refs = refs[len(FRONT[part]):]
    for part in range(parts):
        siblings.append(refs[:len(BACK[part])])
        refs = refs[len(siblings[part]):] if part < parts - 1 else refs
    mixed_ref, squares_ref = refs[-2:]
    core, chip, _, _ = place()
    rows, width = query_ref.shape
    use = use_ref[...]
    squares = jnp.zeros((rows, HD), F32)
    order = steps(width)
    first = len(order) - len(part_steps(width, parts - 1, BACK[-1][-1]))
    for i, step in enumerate(order):
        found = [intras[which][:, tile(at)] for which, at in sources[i]]
        both = found[0] if sources[i][0] == sources[i][1] else jnp.where(core == 0, *found)
        own, part, k, j = step
        size = sizes(width)[part]
        spot = QUARTERS.index(k)
        if own:
            which, at = found_in(FRONT[part], spot)
            state = weight("mix_scale") * states[part][spot][tile(j), :]
            state = state + weight("mix_add") * gots[part][which][tile(at * size + j), :]
            past = from_past(use, query_ref, step, state)
        elif i < first:
            which, at = found_in(BACK[part], spot)
            past = use * siblings[part][which][:, tile(at * size + j)]
        else:
            mixed_ref[:, tile(i)] = both
            continue
        both = both + past
        squares = squares + both * both
        mixed_ref[:, tile(i)] = both * gain_ref[:, column(width, core, chip, *step)]
    squares_ref[...] = squares


def norm_kernel(use_ref, gain_ref, mixed_ref, squares_ref, sibling_ref, out_hbm, out_ref, sems):
    core, chip, _, _ = place()
    rows, width = out_ref.shape
    order = steps(width)
    first = len(order) - sibling_ref.shape[1] // HD
    use = use_ref[...]
    squares = squares_ref[...]
    late = []
    for i, step in enumerate(order[first:]):
        both = mixed_ref[:, tile(first + i)] + use * sibling_ref[:, tile(i)]
        squares = squares + both * both
        late.append(both * gain_ref[:, column(width, core, chip, *step)])
    mean = jnp.sum(squares, axis=-1, keepdims=True) * (1.0 / width)
    norm = jnp.broadcast_to(lax.rsqrt(mean + 1e-05), (rows, HD))
    copies = []
    number = sems.shape[0]
    for part in range(number):
        at = slice(part * rows // number, (part + 1) * rows // number)
        for i, step in enumerate(order):
            both = mixed_ref[at, tile(i)] if i < first else late[i - first][at, :]
            out_ref[at, column(width, core, chip, *step)] = (both * norm[at, :]).astype(BF16)
        copies.append(pltpu.make_async_copy(out_ref.at[at, :], out_hbm.at[at, :], sems.at[part]))
        copies[-1].start()
    for copy in copies:
        copy.wait()


def in_hbm(array):
    return pltpu.with_memory_space_constraint(array, pltpu.HBM)


def array(shape, dtype=F32):
    return jax.ShapeDtypeStruct(shape, dtype)


def shards(count, query_rows, key_rows, value_rows, seg_starts, norm_gain):
    query, key, value = query_rows[0], key_rows[0], value_rows[0]
    rows, width = query.shape
    groups = count // (2 * CHIPS)
    parts = range(len(SPLIT))
    heads = len(steps(width))
    lanes = [array((size * HD, HD)) for size in sizes(width)]

    def tall(part, spots):
        return array((len(part_steps(width, part, spots)) * HD, HD))

    def call(kernel, outs, *args, scratch=()):
        return pl.pallas_call(
            kernel, out_shape=outs, in_specs=[VM] * len(args), out_specs=jax.tree.map(lambda _: VM, outs),
            scratch_shapes=scratch, compiler_params=PARAMS,
        )(*args)

    def weighted(kernel, outs, *args):
        def body(table_ref, *refs):
            return kernel(functools.partial(row, table_ref, groups), *refs)

        return call(body, outs, table, *args)

    def swap(what, bits):
        return lax.ppermute(what, "ctx", [(i, i ^ bits) for i in range(count)])

    def later(what, shift):
        return lax.ppermute(what, "ctx", [(i, (i + shift * 2 * CHIPS) % count) for i in range(count)])

    def intra(on, span, *after):
        out = array((rows, (span[1] - span[0]) * HD))
        return call(functools.partial(intra_kernel, on, span), out, allowed, query, key, value, *after)

    def summary(what, *after):
        outs = [tall(*step[1:]) for step in what]
        return call(functools.partial(summary_kernel, what), outs, kept, key, value, *after)

    some = pltpu.VMEM((rows, sizes(width)[0] * CHIPS * HD), BF16)
    table, kept, allowed, use, *sends = pl.pallas_call(
        functools.partial(first_kernel, groups),
        out_shape=[
            array((-(-len(table_rows(groups)) // 8) * 8, HD)), array((rows, HD), BF16), array((rows, rows)),
            array((rows, HD)), tall(0, range(CHIPS))],
        in_specs=[HB] * 3, out_specs=[VM] * 5,
        scratch_shapes=[
            pltpu.SMEM(seg_starts.shape, jnp.int32), some, some, pltpu.SemaphoreType.DMA((1 + 2 * CHIPS,))],
        compiler_params=PARAMS,
    )(in_hbm(seg_starts), in_hbm(key), in_hbm(value))
    gots, keeps = [], []
    for part in parts:
        gots.append([swap(send, 1) for send in sends])
        keep = [(True, part, spots) for spots in FRONT[part]]
        send = [(False, part + 1, spots) for spots in FRONT[part + 1]] if part + 1 < len(SPLIT) else []
        outs = summary(keep + send)
        keeps.append(outs[:len(keep)])
        sends = outs[len(keep):]
    done = [[None] * heads, [None] * heads]
    intras = []

    def inside(slot, *after):
        new = []
        for on, span in SLOTS.get(slot, ()):
            span = tuple(heads * at // 32 for at in span)
            for core in range(2) if on is None else (on,):
                done[core][slice(*span)] = [(len(intras), i) for i in range(span[1] - span[0])]
            intras.append(intra(on, span, *after))
            new.append(intras[-1])
        return new

    chips, totals, states, siblings = [{} for _ in range(4)]

    def begin(part, *after):
        own = {}
        for spots, keep, got in zip(FRONT[part], keeps[part], gots[part]):
            outs = weighted(
                functools.partial(chip_kernel, len(spots)), [lanes[part]] * len(spots), keep, got, *after)
            own.update(zip(spots, outs))
        chips[part] = {spot: swap(own[spot], 2 * QUARTERS[spot]) if QUARTERS[spot] else own[spot] for spot in own}
        return chips[part]

    def between(part, *after):
        total = weighted(total_kernel, lanes[part], *[chips[part][spot] for spot in range(CHIPS)], *after)
        totals[part] = [later(total, shift) for shift in range(1, groups)]
        return [total]

    def enter(part, *after):
        outs = weighted(
            functools.partial(straight_kernel, groups - 1), [lanes[part]] * CHIPS,
            *[chips[part][spot] for spot in range(CHIPS)], *totals[part], *after)
        states[part] = [swap(out, 2 * k) if k else out for out, k in zip(outs, QUARTERS)]
        return [outs[0]]

    def share(part, *after):
        siblings[part] = []
        for spots in BACK[part]:
            siblings[part].append(swap(weighted(
                functools.partial(pair_kernel, part, spots), array((rows, tall(part, spots).shape[0])), *keeps[part],
                *[states[part][spot] for spot in spots], asked, *after), 1))
        return siblings[part][:1]

    asked = swap(call(query_kernel, array((rows, width // 2)), query), 1)
    a = begin(0, *inside("start", keeps[0][0]))
    b = begin(1, a[1], asked)
    a = between(0, *inside("begin", b[0]))
    b = between(1, *inside("between", a[0]))
    a = enter(0, *inside("between1", b[0]))
    b = enter(1, *inside("enter", a[0]))
    a = share(0, *inside("enter1", b[0]))
    b = share(1, *inside("share", a[0]))
    siblings, states = [siblings[part] for part in parts], [states[part] for part in parts]
    gain = norm_gain[None, :]
    mixed, squares = weighted(
        functools.partial(mix_kernel, list(zip(*done)), len(intras)), [array((rows, width)), array((rows, HD))], use, query, gain,
        *intras, *[piece for state in states for piece in state], *[got for group in gots for got in group],
        *[sibling for group in siblings for sibling in group][:-1])
    attended = pl.pallas_call(
        norm_kernel, out_shape=array((rows, width), BF16), in_specs=[VM] * 5, out_specs=HB,
        scratch_shapes=[pltpu.VMEM((rows, width), BF16), pltpu.SemaphoreType.DMA((4,))], compiler_params=PARAMS,
    )(use, gain, mixed, squares, siblings[-1][-1])
    return attended[None]


def solution(mesh):
    placed = (
        P("sess", "ctx", None),
        P("sess", "ctx", None),
        P("sess", "ctx", None),
        P("sess", None),
        P(),
    )
    return jax.shard_map(
        functools.partial(shards, mesh.shape["ctx"]), mesh=mesh, in_specs=placed,
        out_specs=P("sess", "ctx", None), check_vma=False
    )
```
